256 devices in a mesh: seg: 32 (over x, y, core), node: 8 (over z).
Axes of the slice: x: 4, y: 4, z: 8, core: 2. Of those that a mesh axis runs over, the one named last changes fastest.
Arguments:
- record: float32 [8388608], P(('node', 'seg')), parts along dimension 0, may hold values from -6 to 6
- estimate: float32 [32768, 1024], P(('node', 'seg')), parts along dimension 0, may hold values from -6 to 6
- launch_portion: int32 [4096, 1], P('seg'), may hold values from 0 to 31; in each aligned block of 128 rows (0 to 127, 128 to 255, ...) at most 16 rows name the same one
- launch_offset: int32 [4096], P('seg'), may hold values from 0 to 32767
- threshold: float32 [1], replicated, may hold values from 0.5 to 2
Outputs:
- updated: float32 [32768, 1024], P(('node', 'seg')), parts along dimension 0
- residual: float32 [8388608], P(('node', 'seg')), parts along dimension 0
The draws below stay inside these ranges and needn't reach their ends.
There are 8 independent parts, one for each index of `node`. The reference program is written for one: setup_inputs(seed, part) draws one part's arguments, and reference() takes and returns one part's arrays. A program takes and returns all parts, laid end to end along the dimension named above; an argument that names none is the same for every part. Nothing has to cross between parts.
Inputs may be any that keep to these rules, and one draw needn't show every extreme that they name: `launch_portion`: among the 128 shots of one index of seg, at most 16 fire in one segment, and that many do in some segment of some index.
All inputs are finite; a program needn't handle non-finite values.
Results may differ from the reference program's by a relative error of at most 0.000092.
Values sent between devices are 32-bit elements; how exact they have to be, the bound alone decides.
No kernel may reach another device: no remote copies, remote signals or barrier semaphores. Data moves between devices by JAX's collectives and lax.ppermute only.
A program may use at most 64 MiB of HBM per device.

```python
import math
import jax
import jax.numpy as jnp
import numpy as np
from jax import lax

GATHER_DEPTH = 1024
PATCH = 16
SHOT_DEV = 128
PORTION_COUNT = 32768
SHOTS = 4096
LENGTH = 1048576
CAP = 16
N_SEG = 32


def with_ends(drawn, key, smallest, largest):
    place = [jax.random.randint(jax.random.fold_in(key, axis), (), 0, length) for axis, length in enumerate(drawn.shape)]
    main_axis = drawn.shape.index(max(drawn.shape))
    neighbour = place[:main_axis] + [(place[main_axis] + 1) % drawn.shape[main_axis]] + place[main_axis + 1:]
    return drawn.at[tuple(place)].set(smallest).at[tuple(neighbour)].set(largest)


def block_levels(rng, shape, split, smallest, high):
    factor_of, own = 1.0, jax.random.fold_in(rng, 6)
    for axis_at, blocks in split:
        draws = jnp.exp(jax.random.uniform(jax.random.fold_in(own, axis_at), (blocks,), jnp.float32, smallest / len(split), high / len(split)))
        factor_of = factor_of * jnp.repeat(draws, shape[axis_at] // blocks).reshape([-1 if axis == axis_at else 1 for axis in range(len(shape))])
    return factor_of


def deal_out(own_key, own, number, rows, number_of, top, limit, lean):
    ranking = jax.random.permutation(own_key, number_of)
    crowded, usual = portions_of(number_of, rows * top, limit, lean, True), portions_of(number_of, rows * top, limit, lean, False)
    places = jnp.arange(number_of)

    def named(tallies, turn):
        used = int((tallies > 0).sum())
        fixed = max(1, used // 4)
        passed = fixed + (places - fixed + turn * (used - fixed)) % max(1, number_of - fixed)
        return jnp.zeros((number_of,), jnp.int32).at[ranking[jnp.where(places < fixed, places, passed)]].set(jnp.asarray(tallies, jnp.int32))

    tallies = jnp.where(number % 4 == 0, named(crowded, number // 4), named(usual, number - number // 4 - 1))
    mixed = jax.random.permutation(jax.random.fold_in(own, 3), number_of)
    donor, taker = mixed[0:number_of // 2 * 2:2], mixed[1:number_of // 2 * 2:2]
    slack = jnp.minimum(tallies[donor] - 1, limit - tallies[taker]) // 2
    slack = jnp.where((donor == ranking[0]) | (taker == ranking[0]) | (tallies[taker] == 0), 0, jnp.maximum(slack, 0))
    passed = jax.random.randint(jax.random.fold_in(own, 4), (number_of // 2,), 0, 1 << 20) % (slack + 1)
    tallies = tallies.at[donor].add(-passed).at[taker].add(passed)
    labels = jnp.searchsorted(jnp.cumsum(tallies), jnp.arange(rows * top), side="right").astype(jnp.int32)
    grid = labels.reshape(top, rows).T
    grid = grid[jax.random.permutation(jax.random.fold_in(own, 1), rows)]
    turn = jax.random.randint(jax.random.fold_in(own, 2), (rows, 1), 0, top)
    return jnp.take_along_axis(grid, (jnp.arange(top)[None, :] + turn) % top, axis=1)


def portions_of(amount, total, most, skew, full):
    loads = [(1 << 20) // math.isqrt(rank ** skew) + 1 for rank in range(1, amount + 1)]
    largest = most if full else min(most, max(-(-total // amount), total * loads[0] // sum(loads)))
    least = 1 if total - largest >= amount - 1 else 0
    holding, rest = [largest] + [least] * (amount - 1), total - largest - least * (amount - 1)
    while rest > 0:
        movable = [i for i in range(1, amount) if holding[i] < largest] or [i for i in range(1, amount) if holding[i] < most]
        whole, remaining = sum([loads[i] for i in movable]), rest
        for i in movable:
            addition = min(most - holding[i], max(1, remaining * loads[i] // whole), rest)
            holding[i] = holding[i] + addition
            rest = rest - addition
    return np.array(holding)


def gaussian(stream_key, extent, scale, limit, cuts=(), kind=jnp.bfloat16):
    values = jax.random.normal(stream_key, extent, jnp.float32) * scale
    if len(cuts) > 0:
        values = block_levels(stream_key, extent, cuts, -0.22, 0.18) * values
    return jnp.clip(values, min=-limit, max=limit).astype(kind)


def setup_inputs(seed: int = 0, part: int = 0) -> dict:
    keys = jax.random.split(jax.random.key(seed), 6)
    part_keys = jax.random.split(jax.random.fold_in(keys[5], part), 6)
    record = gaussian(part_keys[0], (LENGTH,), 1.0, 6.0, ((0, 32),), jnp.float32)
    estimate = gaussian(part_keys[1], (SHOTS, GATHER_DEPTH), 1.0, 6.0, ((0, 32),), jnp.float32)
    launch_portion_keys = jax.random.split(jax.random.fold_in(keys[2], 1), SHOTS // SHOT_DEV)
    launch_portion_turns = jax.random.permutation(jax.random.fold_in(keys[2], 3), SHOTS // SHOT_DEV)
    launch_portion = jax.vmap(lambda own, number: deal_out(jax.random.fold_in(keys[2], 2), own, number, SHOT_DEV, N_SEG, 1, CAP, 2))(launch_portion_keys, launch_portion_turns).reshape((SHOTS, 1))
    launch_offset = with_ends(jax.random.randint(keys[3], (SHOTS,), 0, PORTION_COUNT), jax.random.fold_in(keys[3], 1), 0, PORTION_COUNT - 1).astype(jnp.int32)
    threshold = jnp.clip(jax.random.uniform(keys[4], (1,), jnp.float32, 0.5, 2.0), 0.5, 2.0)
    return {"record": record, "estimate": estimate, "launch_portion": launch_portion, "launch_offset": launch_offset, "threshold": threshold}


def tables(count):
    index = jnp.arange(count, dtype=jnp.int32)
    phase = index[:, None] * index[None, :] % count
    angle = phase.astype(jnp.float32) * (2.0 * math.pi / count)
    return (jnp.cos(angle), jnp.sin(angle))

def shrink(stepped, cutoff):
    shot_rows = stepped.shape[0]
    samples = stepped.shape[1]
    high = lax.Precision.HIGHEST
    cos_time, sin_time = tables(samples)
    cos_patch, sin_patch = tables(PATCH)
    scale = 1.0 / math.sqrt(PATCH * samples)

    def mix(table, value):
        return jnp.einsum('qp,npt->nqt', table, value, precision=high)
    real_time = jnp.dot(stepped, cos_time, precision=high, preferred_element_type=jnp.float32)
    imag_time = -jnp.dot(stepped, sin_time, precision=high, preferred_element_type=jnp.float32)
    real_time = real_time.reshape(shot_rows // PATCH, PATCH, samples)
    imag_time = imag_time.reshape(shot_rows // PATCH, PATCH, samples)
    real_part = (mix(cos_patch, real_time) + mix(sin_patch, imag_time)) * scale
    imag_part = (mix(cos_patch, imag_time) - mix(sin_patch, real_time)) * scale
    power = real_part * real_part + imag_part * imag_part
    factor = 1.0 - cutoff * lax.rsqrt(jnp.maximum(power, cutoff * cutoff))
    real_part = real_part * factor
    imag_part = imag_part * factor
    back_real = (mix(cos_patch, real_part) - mix(sin_patch, imag_part)).reshape(shot_rows, samples)
    back_imag = (mix(cos_patch, imag_part) + mix(sin_patch, real_part)).reshape(shot_rows, samples)
    result = jnp.dot(back_real, cos_time, precision=high, preferred_element_type=jnp.float32)
    result = result - jnp.dot(back_imag, sin_time, precision=high, preferred_element_type=jnp.float32)
    return result * scale

def reference(record, estimate, launch_portion, launch_offset, threshold):
    launch_moments = launch_portion[:, 0] * PORTION_COUNT + launch_offset
    launch_spots = launch_moments[:, None] + jnp.arange(GATHER_DEPTH, dtype=jnp.int32)[None, :]
    padded = jnp.zeros((LENGTH + GATHER_DEPTH,), jnp.float32).at[launch_spots].add(estimate)
    residual = record - padded[:LENGTH]
    extended = jnp.concatenate([residual, jnp.zeros((GATHER_DEPTH,), jnp.float32)])
    windowed = extended[launch_spots]
    stepped = estimate + 0.5 * windowed
    return (shrink(stepped, threshold[0]), residual)
```

```python
import math

import jax
import jax.numpy as jnp
import ml_dtypes
import numpy as np
from jax import lax
from jax.experimental import pallas as pl
from jax.experimental.pallas import tpu as pltpu
from jax.sharding import PartitionSpec as P

PATCH = 16
LANES = 128
SIDE = 4
SEGS = 32
SEG_ROWS = 256
SLOT = 280
SHOTS = 128
SAMPLES = 1024
TILES = SAMPLES // LANES
HALF = SAMPLES // 2
F32 = jnp.float32
BF16 = jnp.bfloat16


def seg_index(x, y, core):
    return ((x % SIDE) * SIDE + (y % SIDE)) * 2 + core


def shift_pairs(step, first):
    pairs = []
    for x in range(SIDE):
        for y in range(SIDE):
            for core in range(2):
                along_x = (core == 0) == first
                to = seg_index(x + step, y, core) if along_x else seg_index(x, y + step, core)
                pairs.append((seg_index(x, y, core), to))
    return pairs


def shift(value, step, first):
    return lax.ppermute(value, "seg", shift_pairs(step, first))


def swap_cores(value):
    return lax.ppermute(value, "seg", [(i, i ^ 1) for i in range(SEGS)])


def split(value):
    high = value.astype(BF16)
    return high, (value - high.astype(F32)).astype(BF16)


def np_split(value):
    value = value.astype(np.float32)
    high = value.astype(ml_dtypes.bfloat16)
    return high, (value - high.astype(np.float32)).astype(ml_dtypes.bfloat16)


def time_table():
    sample = np.arange(SAMPLES)
    phase = np.outer(sample, np.arange(HALF)) % SAMPLES
    angle = phase * (2.0 * math.pi / SAMPLES)
    last = np.zeros((SAMPLES, LANES))
    last[:, 0] = 1.0 - 2.0 * (sample % 2)
    return np.concatenate([np.cos(angle), -np.sin(angle), last], axis=1)


def patch_table():
    phase = np.outer(np.arange(PATCH), np.arange(PATCH)) % PATCH
    angle = phase * (2.0 * math.pi / PATCH)
    blocks = np.eye(SHOTS // PATCH)
    cos, sin = np.kron(blocks, np.cos(angle)), np.kron(blocks, np.sin(angle))
    return np.block([[cos, sin], [-sin, cos]])


def place_kernel(base, lane, own, other, *refs):
    outs, (rows, acc, sems) = refs[:SIDE], refs[SIDE:]
    for half, source in enumerate((own, other)):
        for tile in range(TILES):
            rows[pl.ds((half * TILES + tile) * SHOTS, SHOTS), :] = source[:, pl.ds(tile * LANES, LANES)]
    acc[...] = jnp.zeros_like(acc)
    lanes = lax.broadcasted_iota(jnp.int32, (8, LANES), 1)

    for half in range(2):

        def body(i, carry, half=half):
            row = rows[pl.ds(half * SAMPLES + i, TILES, stride=SHOTS), :]
            shot = half * SHOTS + i
            start, turn = base[shot], lane[shot]
            row = pltpu.roll(row, turn, 1)
            here = lanes >= turn
            acc[pl.ds(start, 8), :] += jnp.where(here, row, 0.0)
            acc[pl.ds(start + 1, 8), :] += jnp.where(here, 0.0, row)
            return carry

        lax.fori_loop(0, SHOTS, body, 0, unroll=8)

    copies = []
    for k in range(SIDE):
        for m in range(SIDE):
            slot = k * SIDE + m
            copy = pltpu.make_async_copy(
                acc.at[pl.ds(slot * SLOT + 8, SEG_ROWS)],
                outs[k].at[pl.ds(m * SEG_ROWS, SEG_ROWS)],
                sems.at[slot],
            )
            copy.start()
            copies.append(copy)
    for copy in copies:
        copy.wait()


def place(base, lane, own, other):
    block = jax.ShapeDtypeStruct((SIDE * SEG_ROWS, LANES), F32)
    smem = pl.BlockSpec(memory_space=pltpu.SMEM)
    vmem = pl.BlockSpec(memory_space=pltpu.VMEM)
    return pl.pallas_call(
        place_kernel,
        out_shape=[block] * SIDE,
        in_specs=[smem, smem, vmem, vmem],
        out_specs=[pl.BlockSpec(memory_space=pl.ANY)] * SIDE,
        scratch_shapes=[
            pltpu.VMEM((2 * SAMPLES, LANES), F32),
            pltpu.VMEM((SIDE * SIDE * SLOT + 32, LANES), F32),
            pltpu.SemaphoreType.DMA((SIDE * SIDE,)),
        ],
        compiler_params=pltpu.CompilerParams(vmem_limit_bytes=32 << 20),
        name="place_shots",
    )(base, lane, own, other)


def aims(firing, first, second, core):
    seg, row, lane = firing >> 15, (firing >> 7) & (SEG_ROWS - 1), firing & (LANES - 1)
    inside = (seg & 1) == core
    seg = jnp.where(inside, seg, seg + 1)
    row = jnp.where(inside, row, row - SEG_ROWS)
    kept = inside | ((row >= -8) & (seg < SEGS))
    x, y = seg >> 3, (seg >> 1) & 3
    to_first = jnp.where(core == 0, x, y)
    to_second = jnp.where(core == 0, y, x)
    slot = ((to_first - first) & 3) * SIDE + ((to_second - second) & 3)
    dummy = SIDE * SIDE * SLOT + 8
    return jnp.where(kept, slot * SLOT + 8 + row, dummy), lane


def dot3(a, b):
    out = jnp.dot(a[0], b[0], preferred_element_type=F32)
    out += jnp.dot(a[1], b[0], preferred_element_type=F32)
    return out + jnp.dot(a[0], b[1], preferred_element_type=F32)


def dot3_t(a, b):
    def one(x, y):
        return lax.dot_general(x, y, (((1,), (1,)), ((), ())), preferred_element_type=F32)

    return one(a[0], b[0]) + one(a[1], b[0]) + one(a[0], b[1])


def shrink_kernel(places, firing, cutoff, est, *refs):
    blocks, (time_hi, time_lo, patch_hi, patch_lo, fwd_hi, fwd_lo) = refs[: 2 * SIDE], refs[2 * SIDE : 2 * SIDE + 6]
    out, line, wins, tab_hi, tab_lo, sems, tab_sems = refs[2 * SIDE + 6 :]
    copies = []
    for which in range(2 * SIDE):
        for m in range(SIDE):
            n = which * SIDE + m
            copy = pltpu.make_async_copy(
                blocks[which].at[pl.ds(m * SEG_ROWS, SEG_ROWS)],
                line.at[pl.ds(pl.multiple_of(places[n] * SEG_ROWS, SEG_ROWS), SEG_ROWS)],
                sems.at[n],
            )
            copy.start()
            copies.append(copy)
    tables = [
        pltpu.make_async_copy(time_hi, tab_hi, tab_sems.at[0]),
        pltpu.make_async_copy(time_lo, tab_lo, tab_sems.at[1]),
    ]
    for copy in tables:
        copy.start()
    line[pl.ds(SEGS * SEG_ROWS, 16), :] = jnp.zeros((16, LANES), F32)
    lanes = lax.broadcasted_iota(jnp.int32, (8, LANES), 1)
    for copy in copies:
        copy.wait()

    def body(i, carry):
        start = firing[i]
        row, turn = start >> 7, start & (LANES - 1)
        now = line[pl.ds(row, 8), :]
        later = line[pl.ds(row + 1, 8), :]
        window = jnp.where(lanes >= turn, now, later)
        wins[pl.ds(i, TILES, stride=SHOTS), :] = pltpu.roll(window, (LANES - turn) & (LANES - 1), 1)
        return carry

    lax.fori_loop(0, SHOTS, body, 0, unroll=8)
    stepped = jnp.concatenate(
        [
            est[:, pl.ds(t * LANES, LANES)] + 0.5 * wins[pl.ds(t * SHOTS, SHOTS), :]
            for t in range(TILES)
        ],
        axis=1,
    )
    for copy in tables:
        copy.wait()
    time = (tab_hi[...], tab_lo[...])
    mixed = dot3(split(stepped), time)
    last = mixed[:, 2 * HALF :]
    stacked = jnp.concatenate(
        [
            jnp.concatenate([mixed[:, :HALF], last], axis=1),
            jnp.concatenate([mixed[:, HALF : 2 * HALF], jnp.zeros_like(last)], axis=1),
        ],
        axis=0,
    )
    coeff = dot3((fwd_hi[...], fwd_lo[...]), split(stacked))
    real, imag = coeff[:SHOTS], coeff[SHOTS:]
    level = cutoff[0] * 128.0
    power = real * real + imag * imag
    factor = 1.0 - level * lax.rsqrt(jnp.maximum(power, level * level))
    column = lax.broadcasted_iota(jnp.int32, real.shape, 1)
    weight = jnp.where((column == 0) | (column >= HALF), 1.0, 2.0)
    factor = factor * weight
    shrunk = jnp.concatenate([real * factor, imag * factor], axis=0)
    back = dot3((patch_hi[...], patch_lo[...]), split(shrunk))
    spread = jnp.concatenate([back[:SHOTS, :HALF], back[SHOTS:, :HALF], back[:SHOTS, HALF:]], axis=1)
    out[...] = dot3_t(split(spread), time) * (1.0 / (PATCH * SAMPLES))


def shrink(places, firing, cutoff, est, blocks):
    smem = pl.BlockSpec(memory_space=pltpu.SMEM)
    vmem = pl.BlockSpec(memory_space=pltpu.VMEM)
    anywhere = pl.BlockSpec(memory_space=pl.ANY)
    time = np_split(time_table())
    forward = np_split(patch_table())
    backward = np_split(patch_table().T)
    width = 2 * HALF + LANES
    return pl.pallas_call(
        shrink_kernel,
        out_shape=jax.ShapeDtypeStruct((SHOTS, SAMPLES), F32),
        in_specs=[smem, smem, smem, vmem] + [anywhere] * (2 * SIDE + 2) + [vmem] * 4,
        out_specs=vmem,
        scratch_shapes=[
            pltpu.VMEM((SEGS * SEG_ROWS + 16, LANES), F32),
            pltpu.VMEM((SAMPLES, LANES), F32),
            pltpu.VMEM((SAMPLES, width), BF16),
            pltpu.VMEM((SAMPLES, width), BF16),
            pltpu.SemaphoreType.DMA((SEGS,)),
            pltpu.SemaphoreType.DMA((2,)),
        ],
        compiler_params=pltpu.CompilerParams(vmem_limit_bytes=48 << 20),
        name="take_and_shrink",
    )(places, firing, cutoff, est, *blocks, *time, *backward, *forward)


def shards(record, estimate, launch_portion, launch_offset, threshold):
    index = lax.axis_index("seg")
    core, y, x = index & 1, (index >> 1) & 3, index >> 3
    first, second = jnp.where(core == 0, x, y), jnp.where(core == 0, y, x)
    firing = launch_portion[:, 0] * (SEG_ROWS * LANES) + launch_offset

    other_firing = swap_cores(firing)
    other = swap_cores(estimate)
    base, lane = aims(jnp.concatenate([firing, other_firing]), first, second, core)
    parts = place(base, lane, estimate, other)

    arrived = [shift(parts[k], k, True) for k in range(1, SIDE)]
    summed = parts[0] + arrived[0] + arrived[1] + arrived[2]
    summed = [summed[m * SEG_ROWS : (m + 1) * SEG_ROWS] for m in range(SIDE)]
    arrived = [shift(summed[m], m, False) for m in range(1, SIDE)]
    blended = summed[0] + arrived[0] + arrived[1] + arrived[2]
    residual = record.reshape(SEG_ROWS, LANES) - blended

    column = [residual] + [shift(residual, -m, False) for m in range(1, SIDE)]
    column = jnp.concatenate(column, axis=0)
    mine = [column] + [shift(column, -k, True) for k in range(1, SIDE)]
    theirs = [swap_cores(block) for block in mine]

    near, far = jnp.arange(SIDE)[:, None], jnp.arange(SIDE)[None, :]
    x_of = jnp.where(core == 0, (x + near) & 3, (x + far) & 3)
    y_of = jnp.where(core == 0, (y + far) & 3, (y + near) & 3)
    own_places = (x_of * SIDE + y_of) * 2 + core
    x_of = jnp.where(core == 1, (x + near) & 3, (x + far) & 3)
    y_of = jnp.where(core == 1, (y + far) & 3, (y + near) & 3)
    other_places = (x_of * SIDE + y_of) * 2 + (1 - core)
    places = jnp.concatenate([own_places.reshape(-1), other_places.reshape(-1)])
    updated = shrink(places, firing, threshold, estimate, mine + theirs)
    return (updated, residual.reshape(-1))


def solution(mesh):
    placed = (P(("node", "seg")), P(("node", "seg"), None), P("seg", None), P("seg"), P())
    return jax.shard_map(
        shards,
        mesh=mesh,
        in_specs=placed,
        out_specs=(P(("node", "seg"), None), P(("node", "seg"))),
        check_vma=False,
    )
```

```python
import math

import jax
import jax.numpy as jnp
import ml_dtypes
import numpy as np
from jax import lax
from jax.experimental import pallas as pl
from jax.experimental.pallas import tpu as pltpu
from jax.sharding import PartitionSpec as P

PATCH = 16
LANES = 128
SIDE = 4
SEGS = 32
SEG_ROWS = 256
SLOT = SEG_ROWS + 24
SPARE = SIDE * SIDE * SLOT
SHOTS = 128
BOTH = 2 * SHOTS
UNROLL = 16
SAMPLES = 1024
TILES = SAMPLES // LANES
ODD = 256
PAIR = 128
F32 = jnp.float32
BF16 = jnp.bfloat16


def seg_index(x, y, core):
    return ((x % SIDE) * SIDE + (y % SIDE)) * 2 + core


def shift_pairs(step, first):
    pairs = []
    for x in range(SIDE):
        for y in range(SIDE):
            for core in range(2):
                along_x = (core == 0) == first
                to = seg_index(x + step, y, core) if along_x else seg_index(x, y + step, core)
                pairs.append((seg_index(x, y, core), to))
    return pairs


def shift(value, step, first):
    return lax.ppermute(value, "seg", shift_pairs(step, first))


def swap_cores(value):
    return lax.ppermute(value, "seg", [(i, i ^ 1) for i in range(SEGS)])


def split(value):
    high = value.astype(BF16)
    return high, (value - high.astype(F32)).astype(BF16)


def np_split(value):
    value = value.astype(np.float32)
    high = value.astype(ml_dtypes.bfloat16)
    return high, (value - high.astype(np.float32)).astype(ml_dtypes.bfloat16)


def waves(samples, bins):
    phase = np.outer(np.arange(samples), np.asarray(bins)) % SAMPLES
    angle = phase * (2.0 * math.pi / SAMPLES)
    return [np.cos(angle), -np.sin(angle)]


def time_tables():
    odd = waves(2 * ODD, 2 * np.arange(ODD) + 1)
    mid = waves(2 * PAIR, 4 * np.arange(PAIR) + 2)
    even = waves(2 * PAIR, 4 * np.arange(PAIR))
    last = np.zeros((2 * PAIR, LANES))
    last[:, 0] = 1.0 - 2.0 * (np.arange(2 * PAIR) % 2)
    blank = np.zeros((2 * PAIR, LANES))
    return [np.concatenate(t, axis=1) for t in (odd, mid, even + [last, blank])]


def patch_table():
    phase = np.outer(np.arange(PATCH), np.arange(PATCH)) % PATCH
    angle = phase * (2.0 * math.pi / PATCH)
    blocks = np.eye(SHOTS // PATCH)
    cos, sin = np.kron(blocks, np.cos(angle)), np.kron(blocks, np.sin(angle))
    return np.block([[cos, sin], [-sin, cos]])


def all_tables():
    odd, mid, even = [np_split(table) for table in time_tables()]
    forward, backward = np_split(patch_table()), np_split(patch_table().T)
    patch = np.concatenate([np.concatenate(forward), np.concatenate(backward)], axis=1)
    return np.concatenate([*odd, np.concatenate(mid, axis=1), *even, patch])


def add_shots(base, lane, source, rows, acc, listed):
    acc[...] = jnp.zeros_like(acc)
    for tile in range(TILES):
        rows[pl.ds(tile * SHOTS, SHOTS), :] = source[:, pl.ds(tile * LANES, LANES)]

    def note(shot, count):
        listed[count] = shot
        return count + jnp.where(base[shot] >= 0, 1, 0)

    count = lax.fori_loop(0, SHOTS, note, 0, unroll=8)
    for i in range(UNROLL):
        listed[count + i] = SHOTS
    lanes = lax.broadcasted_iota(jnp.int32, (8, LANES), 1)
    top = lax.broadcasted_iota(jnp.int32, (8, LANES), 0) == 0

    def body(n, carry):
        work = []
        for u in range(UNROLL):
            shot = listed[n * UNROLL + u]
            turn = lane[shot]
            row = pltpu.roll(rows[pl.ds(shot & (SHOTS - 1), TILES, stride=SHOTS), :], turn, 1)
            here = lanes >= turn
            next_row = pltpu.roll(jnp.where(here, 0.0, row), 1, 0)
            low = jnp.where(here, row, 0.0) + jnp.where(top, 0.0, next_row)
            work.append((base[shot], low, jnp.where(top, next_row, 0.0)))
        for start, low, high in work:
            acc[pl.ds(start, 8), :] += low
            acc[pl.ds(start + 8, 8), :] += high
        return carry

    lax.fori_loop(0, (count + UNROLL - 1) // UNROLL, body, 0)


def place_kernel(base, lane, source, acc, rows, listed):
    add_shots(base, lane, source, rows, acc, listed)


def finish_kernel(base, lane, spot, source, placed, record, *refs):
    outs, (rows, acc, listed) = refs[:SIDE], refs[SIDE:]
    add_shots(base, lane, source, rows, acc, listed)
    for k in range(SIDE):
        for m in range(SIDE):
            slot = pl.ds((k * SIDE + m) * SLOT + 8, SEG_ROWS)
            outs[k][pl.ds(m * SEG_ROWS, SEG_ROWS), :] = acc[slot, :] + placed[slot, :]
    own = pl.ds(pl.multiple_of(spot[0] * SEG_ROWS, SEG_ROWS), SEG_ROWS)
    outs[0][own, :] -= record[...]


SLOTS = jax.ShapeDtypeStruct((SPARE + 32, LANES), F32)


def place(base, lane, source):
    smem = pl.BlockSpec(memory_space=pltpu.SMEM)
    vmem = pl.BlockSpec(memory_space=pltpu.VMEM)
    return pl.pallas_call(
        place_kernel,
        out_shape=SLOTS,
        in_specs=[smem, smem, vmem],
        out_specs=vmem,
        scratch_shapes=[pltpu.VMEM((SAMPLES, LANES), F32), pltpu.SMEM((SHOTS + UNROLL,), jnp.int32)],
        compiler_params=pltpu.CompilerParams(vmem_limit_bytes=12 << 20),
        cost_estimate=pl.CostEstimate(flops=1 << 20, bytes_accessed=6 << 20, transcendentals=0),
        name="place_shots",
    )(base, lane, source)


def finish(base, lane, spot, source, placed, record):
    smem = pl.BlockSpec(memory_space=pltpu.SMEM)
    vmem = pl.BlockSpec(memory_space=pltpu.VMEM)
    return pl.pallas_call(
        finish_kernel,
        out_shape=[jax.ShapeDtypeStruct((SIDE * SEG_ROWS, LANES), F32)] * SIDE,
        in_specs=[smem] * 3 + [vmem] * 3,
        out_specs=[vmem] * SIDE,
        scratch_shapes=[
            pltpu.VMEM((SAMPLES, LANES), F32),
            pltpu.VMEM(SLOTS.shape, F32),
            pltpu.SMEM((SHOTS + UNROLL,), jnp.int32),
        ],
        compiler_params=pltpu.CompilerParams(vmem_limit_bytes=16 << 20),
        cost_estimate=pl.CostEstimate(flops=1 << 20, bytes_accessed=6 << 20, transcendentals=0),
        name="finish_shots",
    )(base, lane, spot, source, placed, record)


def aims(firing, first, second, core):
    seg, row = firing >> 15, (firing >> 7) & (SEG_ROWS - 1)
    inside = (seg & 1) == core
    kept = inside | ((row >= SEG_ROWS - 8) & (seg < SEGS - 1))
    seg = jnp.where(inside, seg, seg + 1)
    row = jnp.where(inside, row, row - SEG_ROWS)
    x, y = seg >> 3, (seg >> 1) & 3
    to_first = jnp.where(core == 0, x, y)
    to_second = jnp.where(core == 0, y, x)
    slot = ((to_first - first) & 3) * SIDE + to_second
    base = jnp.where(kept, slot * SLOT + 8 + row, -1)
    base = jnp.concatenate([base, jnp.full((8,), SPARE + 8, jnp.int32)])
    return base, jnp.concatenate([firing & (LANES - 1), jnp.zeros((8,), jnp.int32)])


def times(value, high, low):
    a, b = split(value)
    both = jnp.dot(jnp.concatenate([a, b], axis=0), high[...], preferred_element_type=F32)
    return both[:SHOTS] + both[SHOTS:] + jnp.dot(a, low[...], preferred_element_type=F32)


def times_t(value, high, low):
    def one(x, y):
        return lax.dot_general(x, y, (((1,), (1,)), ((), ())), preferred_element_type=F32)

    a, b = split(value)
    both = one(jnp.concatenate([a, b], axis=0), high[...])
    return both[:SHOTS] + both[SHOTS:] + one(a, low[...])


def mix(table, value):
    a, b = split(value)
    both = jnp.dot(table[...], a, preferred_element_type=F32)
    return both[:BOTH] + both[BOTH:] + jnp.dot(table[pl.ds(0, BOTH), :], b, preferred_element_type=F32)


def shrink_kernel(places, firing, cutoff, est, *refs):
    count = 2 * SIDE
    blocks, (table, out, line, wins) = refs[:count], refs[count:]
    tables = [
        table.at[pl.ds(0, 512), :],
        table.at[pl.ds(512, 512), :],
        table.at[pl.ds(1024, 256), pl.ds(0, 256)],
        table.at[pl.ds(1024, 256), pl.ds(256, 256)],
        table.at[pl.ds(1280, 256), pl.ds(0, 384)],
        table.at[pl.ds(1536, 256), pl.ds(0, 384)],
    ]
    fwd, bwd = table.at[pl.ds(1792, 512), pl.ds(0, 256)], table.at[pl.ds(1792, 512), pl.ds(256, 256)]
    for which in range(count):
        for m in range(SIDE):
            spot = pl.multiple_of(places[which * SIDE + m] * SEG_ROWS, SEG_ROWS)
            line[pl.ds(spot, SEG_ROWS), :] = blocks[which][pl.ds(m * SEG_ROWS, SEG_ROWS), :]
    line[pl.ds(SEGS * SEG_ROWS, 16), :] = jnp.zeros((16, LANES), F32)
    lanes = lax.broadcasted_iota(jnp.int32, (8, LANES), 1)

    def body(i, carry):
        start = firing[i]
        row, turn = start >> 7, start & (LANES - 1)
        now = line[pl.ds(row, 8), :]
        later = line[pl.ds(row + 1, 8), :]
        window = jnp.where(lanes >= turn, now, later)
        wins[pl.ds(i, TILES, stride=SHOTS), :] = pltpu.roll(window, (LANES - turn) & (LANES - 1), 1)
        return carry

    lax.fori_loop(0, SHOTS, body, 0, unroll=32)
    stepped = jnp.concatenate(
        [
            est[:, pl.ds(t * LANES, LANES)] - 0.5 * wins[pl.ds(t * SHOTS, SHOTS), :]
            for t in range(TILES)
        ],
        axis=1,
    )
    front, rear = stepped[:, :512], stepped[:, 512:]
    folded = front + rear
    odd = times(front - rear, tables[0], tables[1])
    mid = times(folded[:, :256] - folded[:, 256:], tables[2], tables[3])
    even = times(folded[:, :256] + folded[:, 256:], tables[4], tables[5])
    last = even[:, 2 * PAIR :]
    stacked = jnp.concatenate(
        [
            jnp.concatenate([odd[:, :ODD], mid[:, :PAIR], even[:, :PAIR], last], axis=1),
            jnp.concatenate(
                [odd[:, ODD:], mid[:, PAIR:], even[:, PAIR : 2 * PAIR], jnp.zeros_like(last)], axis=1
            ),
        ],
        axis=0,
    )
    coeff = mix(fwd, stacked)
    real, imag = coeff[:SHOTS], coeff[SHOTS:]
    level = cutoff[0] * 128.0
    power = real * real + imag * imag
    factor = 1.0 - level * lax.rsqrt(jnp.maximum(power, level * level))
    column = lax.broadcasted_iota(jnp.int32, real.shape, 1)
    weight = jnp.where((column == ODD + PAIR) | (column >= ODD + 2 * PAIR), 1.0, 2.0)
    factor = factor * weight * (1.0 / (PATCH * SAMPLES))
    back = mix(bwd, jnp.concatenate([real * factor, imag * factor], axis=0))
    real, imag = back[:SHOTS], back[SHOTS:]
    odd = times_t(jnp.concatenate([real[:, :ODD], imag[:, :ODD]], axis=1), tables[0], tables[1])
    mid = times_t(
        jnp.concatenate([real[:, ODD : ODD + PAIR], imag[:, ODD : ODD + PAIR]], axis=1),
        tables[2],
        tables[3],
    )
    even = times_t(
        jnp.concatenate(
            [
                real[:, ODD + PAIR : ODD + 2 * PAIR],
                imag[:, ODD + PAIR : ODD + 2 * PAIR],
                real[:, ODD + 2 * PAIR :],
            ],
            axis=1,
        ),
        tables[4],
        tables[5],
    )
    folded = jnp.concatenate([even + mid, even - mid], axis=1)
    out[:, :512] = folded + odd
    out[:, 512:] = folded - odd


def shrink(places, firing, cutoff, est, blocks):
    smem = pl.BlockSpec(memory_space=pltpu.SMEM)
    vmem = pl.BlockSpec(memory_space=pltpu.VMEM)
    table = jnp.asarray(all_tables())
    return pl.pallas_call(
        shrink_kernel,
        out_shape=jax.ShapeDtypeStruct((SHOTS, SAMPLES), F32),
        in_specs=[smem, smem, smem] + [vmem] * (len(blocks) + 2),
        out_specs=vmem,
        scratch_shapes=[
            pltpu.VMEM((SEGS * SEG_ROWS + 16, LANES), F32),
            pltpu.VMEM((SAMPLES, LANES), F32),
        ],
        compiler_params=pltpu.CompilerParams(vmem_limit_bytes=24 << 20),
        cost_estimate=pl.CostEstimate(flops=1 << 29, bytes_accessed=8 << 20, transcendentals=0),
        name="take_and_shrink",
    )(places, firing, cutoff, est, *blocks, table)


def shards(record, estimate, launch_portion, launch_offset, threshold):
    index = lax.axis_index("seg")
    core, y, x = index & 1, (index >> 1) & 3, index >> 3
    first, second = jnp.where(core == 0, x, y), jnp.where(core == 0, y, x)
    firing = launch_portion[:, 0] * (SEG_ROWS * LANES) + launch_offset
    record = record.reshape(SEG_ROWS, LANES)
    spot = second.reshape(1)

    other_firing = swap_cores(firing)
    other = swap_cores(estimate)
    placed = place(*aims(firing, first, second, core), estimate)
    parts = finish(*aims(other_firing, first, second, core), spot, other, placed, record)

    arrived = [shift(parts[k], k, True) for k in (2, 1, 3)]
    column = parts[0] + arrived[0] + arrived[1] + arrived[2]
    arrived = [shift(column, k, False) for k in (2, 1, 3)]
    column = column + arrived[0] + arrived[1] + arrived[2]

    far_blocks = {k: shift(column, -k, True) for k in (2, 1, 3)}
    mine = [column] + [far_blocks[k] for k in range(1, SIDE)]
    theirs = [swap_cores(block) for block in mine]
    residual = -lax.dynamic_slice(column, (second * SEG_ROWS, 0), (SEG_ROWS, LANES))

    near, far = jnp.arange(SIDE)[:, None], jnp.arange(SIDE)[None, :]

    def spots(core):
        x_of = jnp.where(core == 0, (x + near) & 3, far)
        y_of = jnp.where(core == 0, far, (y + near) & 3)
        return ((x_of * SIDE + y_of) * 2 + core).reshape(-1)

    places = jnp.concatenate([spots(core), spots(1 - core)])
    updated = shrink(places, firing, threshold, estimate, mine + theirs)
    return (updated, residual.reshape(-1))


def solution(mesh):
    placed = (P(("node", "seg")), P(("node", "seg"), None), P("seg", None), P("seg"), P())
    return jax.shard_map(
        shards,
        mesh=mesh,
        in_specs=placed,
        out_specs=(P(("node", "seg"), None), P(("node", "seg"))),
        check_vma=False,
    )
```

```python
import math

import jax
import jax.numpy as jnp
import ml_dtypes
import numpy as np
from jax import lax
from jax.experimental import pallas as pl
from jax.experimental.pallas import tpu as pltpu
from jax.sharding import PartitionSpec as P

PATCH = 16
LANES = 128
SIDE = 4
SEGS = 32
SEG_ROWS = 256
SLOT = SEG_ROWS + 24
SPARE = SIDE * SIDE * SLOT
SHOTS = 128
BOTH = 2 * SHOTS
UNROLL = 16
SAMPLES = 1024
TILES = SAMPLES // LANES
ODD = 256
PAIR = 128
F32 = jnp.float32
BF16 = jnp.bfloat16


def seg_index(x, y, core):
    return ((x % SIDE) * SIDE + (y % SIDE)) * 2 + core


def shift_pairs(step, first):
    pairs = []
    for x in range(SIDE):
        for y in range(SIDE):
            for core in range(2):
                along_x = (core == 0) == first
                to = seg_index(x + step, y, core) if along_x else seg_index(x, y + step, core)
                pairs.append((seg_index(x, y, core), to))
    return pairs


def shift(value, step, first):
    return lax.ppermute(value, "seg", shift_pairs(step, first))


def swap_cores(value):
    return lax.ppermute(value, "seg", [(i, i ^ 1) for i in range(SEGS)])


def split(value):
    high = value.astype(BF16)
    return high, (value - high.astype(F32)).astype(BF16)


def np_split(value):
    value = value.astype(np.float32)
    high = value.astype(ml_dtypes.bfloat16)
    return high, (value - high.astype(np.float32)).astype(ml_dtypes.bfloat16)


def waves(samples, bins):
    phase = np.outer(np.arange(samples), np.asarray(bins)) % SAMPLES
    angle = phase * (2.0 * math.pi / SAMPLES)
    return [np.cos(angle), -np.sin(angle)]


def time_tables():
    odd = waves(2 * ODD, 2 * np.arange(ODD) + 1)
    mid = waves(2 * PAIR, 4 * np.arange(PAIR) + 2)
    even = waves(2 * PAIR, 4 * np.arange(PAIR))
    last = np.zeros((2 * PAIR, LANES))
    last[:, 0] = 1.0 - 2.0 * (np.arange(2 * PAIR) % 2)
    blank = np.zeros((2 * PAIR, LANES))
    return [np.concatenate(t, axis=1) for t in (odd, mid, even + [last, blank])]


def patch_table():
    phase = np.outer(np.arange(PATCH), np.arange(PATCH)) % PATCH
    angle = phase * (2.0 * math.pi / PATCH)
    blocks = np.eye(SHOTS // PATCH)
    cos, sin = np.kron(blocks, np.cos(angle)), np.kron(blocks, np.sin(angle))
    return np.block([[cos, sin], [-sin, cos]])


def all_tables():
    odd, mid, even = [np_split(table) for table in time_tables()]
    forward, backward = np_split(patch_table()), np_split(patch_table().T)
    patch = np.concatenate([np.concatenate(forward), np.concatenate(backward)], axis=1)
    return np.concatenate([*odd, np.concatenate(mid, axis=1), *even, patch])


def add_shots(base, lane, source, rows, acc, listed, sems=None):
    copies = []
    for tile in range(TILES):
        part, place = (slice(None), pl.ds(tile * LANES, LANES)), pl.ds(tile * SHOTS, SHOTS)
        if sems is None:
            rows[place, :] = source[part]
        else:
            copies.append(pltpu.make_async_copy(source.at[part], rows.at[place], sems.at[tile]))
            copies[-1].start()
    acc[...] = jnp.zeros_like(acc)

    def note(shot, count):
        listed[count] = shot
        return count + jnp.where(base[shot] >= 0, 1, 0)

    count = lax.fori_loop(0, SHOTS, note, 0, unroll=8)
    for i in range(UNROLL):
        listed[count + i] = SHOTS
    for copy in copies:
        copy.wait()
    lanes = lax.broadcasted_iota(jnp.int32, (8, LANES), 1)
    top = lax.broadcasted_iota(jnp.int32, (8, LANES), 0) == 0

    def body(n, carry):
        work = []
        for u in range(UNROLL):
            shot = listed[n * UNROLL + u]
            turn = lane[shot]
            row = pltpu.roll(rows[pl.ds(shot & (SHOTS - 1), TILES, stride=SHOTS), :], turn, 1)
            here = lanes >= turn
            next_row = pltpu.roll(jnp.where(here, 0.0, row), 1, 0)
            low = jnp.where(here, row, 0.0) + jnp.where(top, 0.0, next_row)
            work.append((base[shot], low, jnp.where(top, next_row, 0.0)))
        for start, low, high in work:
            acc[pl.ds(start, 8), :] += low
            acc[pl.ds(start + 8, 8), :] += high
        return carry

    lax.fori_loop(0, (count + UNROLL - 1) // UNROLL, body, 0)


def place_kernel(base, lane, source, acc, rows, listed, sems):
    add_shots(base, lane, source, rows, acc, listed, sems)


def finish_kernel(base, lane, spot, source, placed, record, *refs):
    outs, (rows, acc, listed) = refs[:SIDE], refs[SIDE:]
    add_shots(base, lane, source, rows, acc, listed)
    for k in range(SIDE):
        for m in range(SIDE):
            slot = pl.ds((k * SIDE + m) * SLOT + 8, SEG_ROWS)
            outs[k][pl.ds(m * SEG_ROWS, SEG_ROWS), :] = acc[slot, :] + placed[slot, :]
    own = pl.ds(pl.multiple_of(spot[0] * SEG_ROWS, SEG_ROWS), SEG_ROWS)
    outs[0][own, :] -= record[...]


SLOTS = jax.ShapeDtypeStruct((SPARE + 32, LANES), F32)


def place(base, lane, source):
    smem = pl.BlockSpec(memory_space=pltpu.SMEM)
    vmem = pl.BlockSpec(memory_space=pltpu.VMEM)
    return pl.pallas_call(
        place_kernel,
        out_shape=SLOTS,
        in_specs=[smem, smem, pl.BlockSpec(memory_space=pltpu.HBM)],
        out_specs=vmem,
        scratch_shapes=[
            pltpu.VMEM((SAMPLES, LANES), F32),
            pltpu.SMEM((SHOTS + UNROLL,), jnp.int32),
            pltpu.SemaphoreType.DMA((TILES,)),
        ],
        compiler_params=pltpu.CompilerParams(vmem_limit_bytes=6 << 20),
        cost_estimate=pl.CostEstimate(flops=1 << 20, bytes_accessed=6 << 20, transcendentals=0),
        name="place_shots",
    )(base, lane, pltpu.with_memory_space_constraint(source, pltpu.HBM))


def finish(base, lane, spot, source, placed, record):
    smem = pl.BlockSpec(memory_space=pltpu.SMEM)
    vmem = pl.BlockSpec(memory_space=pltpu.VMEM)
    return pl.pallas_call(
        finish_kernel,
        out_shape=[jax.ShapeDtypeStruct((SIDE * SEG_ROWS, LANES), F32)] * SIDE,
        in_specs=[smem] * 3 + [vmem] * 3,
        out_specs=[vmem] * SIDE,
        scratch_shapes=[
            pltpu.VMEM((SAMPLES, LANES), F32),
            pltpu.VMEM(SLOTS.shape, F32),
            pltpu.SMEM((SHOTS + UNROLL,), jnp.int32),
        ],
        compiler_params=pltpu.CompilerParams(vmem_limit_bytes=10 << 20),
        cost_estimate=pl.CostEstimate(flops=1 << 20, bytes_accessed=6 << 20, transcendentals=0),
        name="finish_shots",
    )(base, lane, spot, source, placed, record)


def aims(firing, first, second, core):
    seg, row = firing >> 15, (firing >> 7) & (SEG_ROWS - 1)
    inside = (seg & 1) == core
    kept = inside | ((row >= SEG_ROWS - 8) & (seg < SEGS - 1))
    seg = jnp.where(inside, seg, seg + 1)
    row = jnp.where(inside, row, row - SEG_ROWS)
    x, y = seg >> 3, (seg >> 1) & 3
    to_first = jnp.where(core == 0, x, y)
    to_second = jnp.where(core == 0, y, x)
    slot = ((to_first - first) & 3) * SIDE + to_second
    base = jnp.where(kept, slot * SLOT + 8 + row, -1)
    base = jnp.concatenate([base, jnp.full((8,), SPARE + 8, jnp.int32)])
    return base, jnp.concatenate([firing & (LANES - 1), jnp.zeros((8,), jnp.int32)])


def times(value, high, low):
    a, b = split(value)
    both = jnp.dot(jnp.concatenate([a, b], axis=0), high[...], preferred_element_type=F32)
    return both[:SHOTS] + both[SHOTS:] + jnp.dot(a, low[...], preferred_element_type=F32)


def times_t(value, high, low):
    def one(x, y):
        return lax.dot_general(x, y, (((1,), (1,)), ((), ())), preferred_element_type=F32)

    a, b = split(value)
    both = one(jnp.concatenate([a, b], axis=0), high[...])
    return both[:SHOTS] + both[SHOTS:] + one(a, low[...])


def mix(table, value):
    a, b = split(value)
    both = jnp.dot(table[...], a, preferred_element_type=F32)
    return both[:BOTH] + both[BOTH:] + jnp.dot(table[pl.ds(0, BOTH), :], b, preferred_element_type=F32)


def cut_windows(base, lane, slots, wins):
    lanes = lax.broadcasted_iota(jnp.int32, (8, LANES), 1)

    def body(i, carry):
        start, turn = base[i], lane[i]
        start = jnp.where(start < 0, SPARE, start)
        window = jnp.where(lanes >= turn, slots[pl.ds(start, 8), :], slots[pl.ds(start + 1, 8), :])
        wins[pl.ds(i, TILES, stride=SHOTS), :] = pltpu.roll(window, (LANES - turn) & (LANES - 1), 1)
        return carry

    lax.fori_loop(0, SHOTS, body, 0, unroll=32)


def cut_kernel(base, lane, spot, *refs):
    blocks, (wins, *residual, slots) = refs[:SIDE], refs[SIDE:]
    slots[pl.ds(0, 8), :] = jnp.zeros((8, LANES), F32)
    for k in range(SIDE):
        for m in range(SIDE):
            start = (k * SIDE + m) * SLOT + 8
            slots[pl.ds(start, SEG_ROWS), :] = blocks[k][pl.ds(m * SEG_ROWS, SEG_ROWS), :]
            slots[pl.ds(start + SEG_ROWS, 24), :] = jnp.zeros((24, LANES), F32)
    slots[pl.ds(SPARE, 32), :] = jnp.zeros((32, LANES), F32)
    if residual:
        own = pl.ds(pl.multiple_of(spot[0] * SEG_ROWS, SEG_ROWS), SEG_ROWS)
        residual[0][...] = -blocks[0][own, :]
    cut_windows(base, lane, slots, wins)


def cut(base, lane, spot, blocks, own):
    smem = pl.BlockSpec(memory_space=pltpu.SMEM)
    vmem = pl.BlockSpec(memory_space=pltpu.VMEM)
    return pl.pallas_call(
        cut_kernel,
        out_shape=[jax.ShapeDtypeStruct((rows, LANES), F32) for rows in (SAMPLES, SEG_ROWS)[: 1 + own]],
        in_specs=[smem, smem, smem] + [vmem] * SIDE,
        out_specs=[vmem] * (1 + own),
        scratch_shapes=[pltpu.VMEM(SLOTS.shape, F32)],
        compiler_params=pltpu.CompilerParams(vmem_limit_bytes=8 << 20),
        cost_estimate=pl.CostEstimate(flops=1 << 20, bytes_accessed=6 << 20, transcendentals=0),
        name="cut_own_windows" if own else "cut_other_windows",
    )(base, lane, spot, *blocks)


def shrink_kernel(cutoff, est, here, there, table, out):
    tables = [
        table.at[pl.ds(0, 512), :],
        table.at[pl.ds(512, 512), :],
        table.at[pl.ds(1024, 256), pl.ds(0, 256)],
        table.at[pl.ds(1024, 256), pl.ds(256, 256)],
        table.at[pl.ds(1280, 256), pl.ds(0, 384)],
        table.at[pl.ds(1536, 256), pl.ds(0, 384)],
    ]
    fwd, bwd = table.at[pl.ds(1792, 512), pl.ds(0, 256)], table.at[pl.ds(1792, 512), pl.ds(256, 256)]
    stepped = jnp.concatenate(
        [
            est[:, pl.ds(t * LANES, LANES)] - 0.5 * (here[pl.ds(t * SHOTS, SHOTS), :] + there[pl.ds(t * SHOTS, SHOTS), :])
            for t in range(TILES)
        ],
        axis=1,
    )
    front, rear = stepped[:, :512], stepped[:, 512:]
    folded = front + rear
    odd = times(front - rear, tables[0], tables[1])
    mid = times(folded[:, :256] - folded[:, 256:], tables[2], tables[3])
    even = times(folded[:, :256] + folded[:, 256:], tables[4], tables[5])
    last = even[:, 2 * PAIR :]
    stacked = jnp.concatenate(
        [
            jnp.concatenate([odd[:, :ODD], mid[:, :PAIR], even[:, :PAIR], last], axis=1),
            jnp.concatenate(
                [odd[:, ODD:], mid[:, PAIR:], even[:, PAIR : 2 * PAIR], jnp.zeros_like(last)], axis=1
            ),
        ],
        axis=0,
    )
    coeff = mix(fwd, stacked)
    real, imag = coeff[:SHOTS], coeff[SHOTS:]
    level = cutoff[0] * 128.0
    power = real * real + imag * imag
    factor = 1.0 - level * lax.rsqrt(jnp.maximum(power, level * level))
    column = lax.broadcasted_iota(jnp.int32, real.shape, 1)
    weight = jnp.where((column == ODD + PAIR) | (column >= ODD + 2 * PAIR), 1.0, 2.0)
    factor = factor * weight * (1.0 / (PATCH * SAMPLES))
    back = mix(bwd, jnp.concatenate([real * factor, imag * factor], axis=0))
    real, imag = back[:SHOTS], back[SHOTS:]
    odd = times_t(jnp.concatenate([real[:, :ODD], imag[:, :ODD]], axis=1), tables[0], tables[1])
    mid = times_t(
        jnp.concatenate([real[:, ODD : ODD + PAIR], imag[:, ODD : ODD + PAIR]], axis=1),
        tables[2],
        tables[3],
    )
    even = times_t(
        jnp.concatenate(
            [
                real[:, ODD + PAIR : ODD + 2 * PAIR],
                imag[:, ODD + PAIR : ODD + 2 * PAIR],
                real[:, ODD + 2 * PAIR :],
            ],
            axis=1,
        ),
        tables[4],
        tables[5],
    )
    folded = jnp.concatenate([even + mid, even - mid], axis=1)
    out[:, :512] = folded + odd
    out[:, 512:] = folded - odd


def shrink(cutoff, est, here, there):
    vmem = pl.BlockSpec(memory_space=pltpu.VMEM)
    return pl.pallas_call(
        shrink_kernel,
        out_shape=jax.ShapeDtypeStruct((SHOTS, SAMPLES), F32),
        in_specs=[pl.BlockSpec(memory_space=pltpu.SMEM)] + [vmem] * 4,
        out_specs=vmem,
        compiler_params=pltpu.CompilerParams(vmem_limit_bytes=12 << 20),
        cost_estimate=pl.CostEstimate(flops=1 << 29, bytes_accessed=8 << 20, transcendentals=0),
        name="shrink",
    )(cutoff, est, here, there, jnp.asarray(all_tables()))


def shards(record, estimate, launch_portion, launch_offset, threshold):
    index = lax.axis_index("seg")
    core, y, x = index & 1, (index >> 1) & 3, index >> 3
    first, second = jnp.where(core == 0, x, y), jnp.where(core == 0, y, x)
    firing = launch_portion[:, 0] * (SEG_ROWS * LANES) + launch_offset
    record = record.reshape(SEG_ROWS, LANES)
    spot = second.reshape(1)

    other_firing = swap_cores(firing)
    other = swap_cores(estimate)
    own_aims = aims(firing, first, second, core)
    other_aims = aims(other_firing, first, second, core)
    placed = place(*own_aims, estimate)
    parts = finish(*other_aims, spot, other, placed, record)

    arrived = [shift(parts[k], k, True) for k in (2, 1, 3)]
    column = parts[0] + arrived[0] + arrived[1] + arrived[2]
    arrived = [shift(column, k, False) for k in (2, 1, 3)]
    column = column + arrived[0] + arrived[1] + arrived[2]

    far_blocks = {k: shift(column, -k, True) for k in (2, 1, 3)}

    blocks = [column] + [far_blocks[k] for k in range(1, SIDE)]
    there = swap_cores(cut(*other_aims, spot, blocks, False)[0])
    here, residual = cut(*own_aims, spot, blocks, True)
    updated = shrink(threshold, estimate, here, there)
    return (updated, residual.reshape(-1))


def solution(mesh):
    placed = (P(("node", "seg")), P(("node", "seg"), None), P("seg", None), P("seg"), P())
    return jax.shard_map(
        shards,
        mesh=mesh,
        in_specs=placed,
        out_specs=(P(("node", "seg"), None), P(("node", "seg"))),
        check_vma=False,
    )
```

```python
import math

import jax
import jax.numpy as jnp
import ml_dtypes
import numpy as np
from jax import lax
from jax.experimental import pallas as pl
from jax.experimental.pallas import tpu as pltpu
from jax.sharding import PartitionSpec as P

PATCH = 16
LANES = 128
SIDE = 4
SEGS = 32
SEG_ROWS = 256
SLOT = SEG_ROWS + 24
SPARE = SIDE * SIDE * SLOT
SHOTS = 128
BOTH = 2 * SHOTS
UNROLL = 16
SAMPLES = 1024
TILES = SAMPLES // LANES
ODD = 256
PAIR = 128
F32 = jnp.float32
BF16 = jnp.bfloat16


def seg_index(x, y, core):
    return ((x % SIDE) * SIDE + (y % SIDE)) * 2 + core


def shift_pairs(step, first):
    pairs = []
    for x in range(SIDE):
        for y in range(SIDE):
            for core in range(2):
                along_x = (core == 0) == first
                to = seg_index(x + step, y, core) if along_x else seg_index(x, y + step, core)
                pairs.append((seg_index(x, y, core), to))
    return pairs


def shift(value, step, first):
    return lax.ppermute(value, "seg", shift_pairs(step, first))


def swap_cores(value):
    return lax.ppermute(value, "seg", [(i, i ^ 1) for i in range(SEGS)])


def split(value):
    high = value.astype(BF16)
    return high, (value - high.astype(F32)).astype(BF16)


def np_split(value):
    value = value.astype(np.float32)
    high = value.astype(ml_dtypes.bfloat16)
    return high, (value - high.astype(np.float32)).astype(ml_dtypes.bfloat16)


def waves(samples, bins):
    phase = np.outer(np.arange(samples), np.asarray(bins)) % SAMPLES
    angle = phase * (2.0 * math.pi / SAMPLES)
    return [np.cos(angle), -np.sin(angle)]


def time_tables():
    odd = waves(2 * ODD, 2 * np.arange(ODD) + 1)
    mid = waves(2 * PAIR, 4 * np.arange(PAIR) + 2)
    even = waves(2 * PAIR, 4 * np.arange(PAIR))
    last = np.zeros((2 * PAIR, LANES))
    last[:, 0] = 1.0 - 2.0 * (np.arange(2 * PAIR) % 2)
    blank = np.zeros((2 * PAIR, LANES))
    return [np.concatenate(t, axis=1) for t in (odd, mid, even + [last, blank])]


def patch_table():
    phase = np.outer(np.arange(PATCH), np.arange(PATCH)) % PATCH
    angle = phase * (2.0 * math.pi / PATCH)
    blocks = np.eye(SHOTS // PATCH)
    cos, sin = np.kron(blocks, np.cos(angle)), np.kron(blocks, np.sin(angle))
    return np.block([[cos, sin], [-sin, cos]])


def all_tables():
    odd, mid, even = [np_split(table) for table in time_tables()]
    forward, backward = np_split(patch_table()), np_split(patch_table().T)
    patch = np.concatenate([np.concatenate(forward), np.concatenate(backward)], axis=1)
    return np.concatenate([*odd, np.concatenate(mid, axis=1), *even, patch])


def add_shots(base, lane, source, rows, acc, listed, sems=None):
    copies = []
    for tile in range(TILES):
        part, place = (slice(None), pl.ds(tile * LANES, LANES)), pl.ds(tile * SHOTS, SHOTS)
        if sems is None:
            rows[place, :] = source[part]
        else:
            copies.append(pltpu.make_async_copy(source.at[part], rows.at[place], sems.at[tile]))
            copies[-1].start()
    acc[...] = jnp.zeros_like(acc)

    def note(shot, count):
        listed[count] = shot
        return count + jnp.where(base[shot] >= 0, 1, 0)

    count = lax.fori_loop(0, SHOTS, note, 0, unroll=8)
    for i in range(UNROLL):
        listed[count + i] = SHOTS
    for copy in copies:
        copy.wait()
    lanes = lax.broadcasted_iota(jnp.int32, (8, LANES), 1)
    top = lax.broadcasted_iota(jnp.int32, (8, LANES), 0) == 0

    def body(n, carry):
        work = []
        for u in range(UNROLL):
            shot = listed[n * UNROLL + u]
            turn = lane[shot]
            row = pltpu.roll(rows[pl.ds(shot & (SHOTS - 1), TILES, stride=SHOTS), :], turn, 1)
            here = lanes >= turn
            next_row = pltpu.roll(jnp.where(here, 0.0, row), 1, 0)
            low = jnp.where(here, row, 0.0) + jnp.where(top, 0.0, next_row)
            work.append((base[shot], low, jnp.where(top, next_row, 0.0)))
        for start, low, high in work:
            acc[pl.ds(start, 8), :] += low
            acc[pl.ds(start + 8, 8), :] += high
        return carry

    lax.fori_loop(0, (count + UNROLL - 1) // UNROLL, body, 0)


def place_kernel(base, lane, source, acc, rows, listed, sems):
    add_shots(base, lane, source, rows, acc, listed, sems)


def finish_kernel(base, lane, spot, source, placed, record, *refs):
    outs, (rows, acc, listed) = refs[:SIDE], refs[SIDE:]
    add_shots(base, lane, source, rows, acc, listed)
    for k in range(SIDE):
        for m in range(SIDE):
            slot = pl.ds((k * SIDE + m) * SLOT + 8, SEG_ROWS)
            outs[k][pl.ds(m * SEG_ROWS, SEG_ROWS), :] = acc[slot, :] + placed[slot, :]
    own = pl.ds(pl.multiple_of(spot[0] * SEG_ROWS, SEG_ROWS), SEG_ROWS)
    outs[0][own, :] -= record[...]


SLOTS = jax.ShapeDtypeStruct((SPARE + 32, LANES), F32)


def place(base, lane, source):
    smem = pl.BlockSpec(memory_space=pltpu.SMEM)
    vmem = pl.BlockSpec(memory_space=pltpu.VMEM)
    return pl.pallas_call(
        place_kernel,
        out_shape=SLOTS,
        in_specs=[smem, smem, pl.BlockSpec(memory_space=pltpu.HBM)],
        out_specs=vmem,
        scratch_shapes=[
            pltpu.VMEM((SAMPLES, LANES), F32),
            pltpu.SMEM((SHOTS + UNROLL,), jnp.int32),
            pltpu.SemaphoreType.DMA((TILES,)),
        ],
        compiler_params=pltpu.CompilerParams(vmem_limit_bytes=6 << 20),
        cost_estimate=pl.CostEstimate(flops=1 << 20, bytes_accessed=6 << 20, transcendentals=0),
        name="place_shots",
    )(base, lane, pltpu.with_memory_space_constraint(source, pltpu.HBM))


def finish(base, lane, spot, source, placed, record):
    smem = pl.BlockSpec(memory_space=pltpu.SMEM)
    vmem = pl.BlockSpec(memory_space=pltpu.VMEM)
    return pl.pallas_call(
        finish_kernel,
        out_shape=[jax.ShapeDtypeStruct((SIDE * SEG_ROWS, LANES), F32)] * SIDE,
        in_specs=[smem] * 3 + [vmem] * 3,
        out_specs=[vmem] * SIDE,
        scratch_shapes=[
            pltpu.VMEM((SAMPLES, LANES), F32),
            pltpu.VMEM(SLOTS.shape, F32),
            pltpu.SMEM((SHOTS + UNROLL,), jnp.int32),
        ],
        compiler_params=pltpu.CompilerParams(vmem_limit_bytes=10 << 20),
        cost_estimate=pl.CostEstimate(flops=1 << 20, bytes_accessed=6 << 20, transcendentals=0),
        name="finish_shots",
    )(base, lane, spot, source, placed, record)


def aims(firing, first, second, core):
    seg, row = firing >> 15, (firing >> 7) & (SEG_ROWS - 1)
    inside = (seg & 1) == core
    kept = inside | ((row >= SEG_ROWS - 8) & (seg < SEGS - 1))
    seg = jnp.where(inside, seg, seg + 1)
    row = jnp.where(inside, row, row - SEG_ROWS)
    x, y = seg >> 3, (seg >> 1) & 3
    to_first = jnp.where(core == 0, x, y)
    to_second = jnp.where(core == 0, y, x)
    slot = ((to_first - first) & 3) * SIDE + to_second
    base = jnp.where(kept, slot * SLOT + 8 + row, -1)
    base = jnp.concatenate([base, jnp.full((8,), SPARE + 8, jnp.int32)])
    return base, jnp.concatenate([firing & (LANES - 1), jnp.zeros((8,), jnp.int32)])


def times(value, high, low):
    a, b = split(value)
    both = jnp.dot(jnp.concatenate([a, b], axis=0), high[...], preferred_element_type=F32)
    return both[:SHOTS] + both[SHOTS:] + jnp.dot(a, low[...], preferred_element_type=F32)


def times_t(value, high, low):
    def one(x, y):
        return lax.dot_general(x, y, (((1,), (1,)), ((), ())), preferred_element_type=F32)

    a, b = split(value)
    both = one(jnp.concatenate([a, b], axis=0), high[...])
    return both[:SHOTS] + both[SHOTS:] + one(a, low[...])


def mix(table, value):
    a, b = split(value)
    both = jnp.dot(table[...], a, preferred_element_type=F32)
    return both[:BOTH] + both[BOTH:] + jnp.dot(table[pl.ds(0, BOTH), :], b, preferred_element_type=F32)


def side_kernel(spot, own_base, other_base, column, residual, own_list, other_list):
    own = pl.ds(pl.multiple_of(spot[0] * SEG_ROWS, SEG_ROWS), SEG_ROWS)
    residual[...] = -column[own, :]
    for base, listed in ((own_base, own_list), (other_base, other_list)):

        def note(shot, count, base=base, listed=listed):
            listed[count] = shot
            return count + jnp.where(base[shot] >= 0, 1, 0)

        count = lax.fori_loop(0, SHOTS, note, 1, unroll=8)
        for i in range(UNROLL):
            listed[count + i] = listed[jnp.maximum(count - 1, 1)]
        listed[0] = count - 1


def side(spot, own_base, other_base, column):
    smem = pl.BlockSpec(memory_space=pltpu.SMEM)
    vmem = pl.BlockSpec(memory_space=pltpu.VMEM)
    listed = jax.ShapeDtypeStruct((SHOTS + UNROLL + 8,), jnp.int32)
    return pl.pallas_call(
        side_kernel,
        out_shape=[jax.ShapeDtypeStruct((SEG_ROWS, LANES), F32), listed, listed],
        in_specs=[smem, smem, smem, vmem],
        out_specs=[vmem, smem, smem],
        compiler_params=pltpu.CompilerParams(vmem_limit_bytes=2 << 20),
        cost_estimate=pl.CostEstimate(flops=1 << 20, bytes_accessed=8 << 20, transcendentals=0),
        name="residual_and_lists",
    )(spot, own_base, other_base, column)


def cut_kernel(base, lane, listed, *refs):
    blocks, (wins, slots) = refs[:SIDE], refs[SIDE:]
    wins[...] = jnp.zeros_like(wins)
    slots[pl.ds(0, 8), :] = jnp.zeros((8, LANES), F32)
    for k in range(SIDE):
        for m in range(SIDE):
            start = (k * SIDE + m) * SLOT + 8
            slots[pl.ds(start, SEG_ROWS), :] = blocks[k][pl.ds(m * SEG_ROWS, SEG_ROWS), :]
            slots[pl.ds(start + SEG_ROWS, 24), :] = jnp.zeros((24, LANES), F32)
    lanes = lax.broadcasted_iota(jnp.int32, (8, LANES), 1)

    def body(n, carry):
        work = []
        for u in range(UNROLL):
            shot = listed[1 + n * UNROLL + u]
            start, turn = base[shot], lane[shot]
            window = jnp.where(lanes >= turn, slots[pl.ds(start, 8), :], slots[pl.ds(start + 1, 8), :])
            work.append((shot, pltpu.roll(window, (LANES - turn) & (LANES - 1), 1)))
        for shot, window in work:
            wins[pl.ds(shot, TILES, stride=SHOTS), :] = window
        return carry

    lax.fori_loop(0, (listed[0] + UNROLL - 1) // UNROLL, body, 0)


def cut(base, lane, listed, blocks, name):
    smem = pl.BlockSpec(memory_space=pltpu.SMEM)
    vmem = pl.BlockSpec(memory_space=pltpu.VMEM)
    return pl.pallas_call(
        cut_kernel,
        out_shape=jax.ShapeDtypeStruct((SAMPLES, LANES), F32),
        in_specs=[smem, smem, smem] + [vmem] * SIDE,
        out_specs=vmem,
        scratch_shapes=[pltpu.VMEM(SLOTS.shape, F32)],
        compiler_params=pltpu.CompilerParams(vmem_limit_bytes=8 << 20),
        cost_estimate=pl.CostEstimate(flops=1 << 20, bytes_accessed=6 << 20, transcendentals=0),
        name=name,
    )(base, lane, listed, *blocks)


def shrink_kernel(cutoff, est, here, there, table, out):
    tables = [
        table.at[pl.ds(0, 512), :],
        table.at[pl.ds(512, 512), :],
        table.at[pl.ds(1024, 256), pl.ds(0, 256)],
        table.at[pl.ds(1024, 256), pl.ds(256, 256)],
        table.at[pl.ds(1280, 256), pl.ds(0, 384)],
        table.at[pl.ds(1536, 256), pl.ds(0, 384)],
    ]
    fwd, bwd = table.at[pl.ds(1792, 512), pl.ds(0, 256)], table.at[pl.ds(1792, 512), pl.ds(256, 256)]
    stepped = jnp.concatenate(
        [
            est[:, pl.ds(t * LANES, LANES)] - 0.5 * (here[pl.ds(t * SHOTS, SHOTS), :] + there[pl.ds(t * SHOTS, SHOTS), :])
            for t in range(TILES)
        ],
        axis=1,
    )
    front, rear = stepped[:, :512], stepped[:, 512:]
    folded = front + rear
    odd = times(front - rear, tables[0], tables[1])
    mid = times(folded[:, :256] - folded[:, 256:], tables[2], tables[3])
    even = times(folded[:, :256] + folded[:, 256:], tables[4], tables[5])
    last = even[:, 2 * PAIR :]
    stacked = jnp.concatenate(
        [
            jnp.concatenate([odd[:, :ODD], mid[:, :PAIR], even[:, :PAIR], last], axis=1),
            jnp.concatenate(
                [odd[:, ODD:], mid[:, PAIR:], even[:, PAIR : 2 * PAIR], jnp.zeros_like(last)], axis=1
            ),
        ],
        axis=0,
    )
    coeff = mix(fwd, stacked)
    real, imag = coeff[:SHOTS], coeff[SHOTS:]
    level = cutoff[0] * 128.0
    power = real * real + imag * imag
    factor = 1.0 - level * lax.rsqrt(jnp.maximum(power, level * level))
    column = lax.broadcasted_iota(jnp.int32, real.shape, 1)
    weight = jnp.where((column == ODD + PAIR) | (column >= ODD + 2 * PAIR), 1.0, 2.0)
    factor = factor * weight * (1.0 / (PATCH * SAMPLES))
    back = mix(bwd, jnp.concatenate([real * factor, imag * factor], axis=0))
    real, imag = back[:SHOTS], back[SHOTS:]
    odd = times_t(jnp.concatenate([real[:, :ODD], imag[:, :ODD]], axis=1), tables[0], tables[1])
    mid = times_t(
        jnp.concatenate([real[:, ODD : ODD + PAIR], imag[:, ODD : ODD + PAIR]], axis=1),
        tables[2],
        tables[3],
    )
    even = times_t(
        jnp.concatenate(
            [
                real[:, ODD + PAIR : ODD + 2 * PAIR],
                imag[:, ODD + PAIR : ODD + 2 * PAIR],
                real[:, ODD + 2 * PAIR :],
            ],
            axis=1,
        ),
        tables[4],
        tables[5],
    )
    folded = jnp.concatenate([even + mid, even - mid], axis=1)
    out[:, :512] = folded + odd
    out[:, 512:] = folded - odd


def shrink(cutoff, est, here, there):
    vmem = pl.BlockSpec(memory_space=pltpu.VMEM)
    return pl.pallas_call(
        shrink_kernel,
        out_shape=jax.ShapeDtypeStruct((SHOTS, SAMPLES), F32),
        in_specs=[pl.BlockSpec(memory_space=pltpu.SMEM)] + [vmem] * 4,
        out_specs=vmem,
        compiler_params=pltpu.CompilerParams(vmem_limit_bytes=12 << 20),
        cost_estimate=pl.CostEstimate(flops=1 << 29, bytes_accessed=8 << 20, transcendentals=0),
        name="shrink",
    )(cutoff, est, here, there, jnp.asarray(all_tables()))


def shards(record, estimate, launch_portion, launch_offset, threshold):
    index = lax.axis_index("seg")
    core, y, x = index & 1, (index >> 1) & 3, index >> 3
    first, second = jnp.where(core == 0, x, y), jnp.where(core == 0, y, x)
    firing = launch_portion[:, 0] * (SEG_ROWS * LANES) + launch_offset
    record = record.reshape(SEG_ROWS, LANES)
    spot = second.reshape(1)

    other_firing = swap_cores(firing)
    other = swap_cores(estimate)
    own_aims = aims(firing, first, second, core)
    other_aims = aims(other_firing, first, second, core)
    placed = place(*own_aims, estimate)
    parts = finish(*other_aims, spot, other, placed, record)

    arrived = [shift(parts[k], k, True) for k in (2, 1, 3)]
    column = parts[0] + arrived[0] + arrived[1] + arrived[2]
    arrived = [shift(column, k, False) for k in (2, 1, 3)]
    column = column + arrived[0] + arrived[1] + arrived[2]

    residual, own_list, other_list = side(spot, own_aims[0], other_aims[0], column)
    far_blocks = {k: shift(column, -k, True) for k in (2, 1, 3)}

    blocks = [column] + [far_blocks[k] for k in range(1, SIDE)]
    there = swap_cores(cut(*other_aims, other_list, blocks, "cut_other_windows"))
    here = cut(*own_aims, own_list, blocks, "cut_own_windows")
    updated = shrink(threshold, estimate, here, there)
    return (updated, residual.reshape(-1))


def solution(mesh):
    placed = (P(("node", "seg")), P(("node", "seg"), None), P("seg", None), P("seg"), P())
    return jax.shard_map(
        shards,
        mesh=mesh,
        in_specs=placed,
        out_specs=(P(("node", "seg"), None), P(("node", "seg"))),
        check_vma=False,
    )
```

```python
import math

import jax
import jax.numpy as jnp
import ml_dtypes
import numpy as np
from jax import lax
from jax.experimental import pallas as pl
from jax.experimental.pallas import tpu as pltpu
from jax.sharding import PartitionSpec as P

PATCH = 16
LANES = 128
SIDE = 4
SEGS = 32
SEG_ROWS = 256
SLOT = SEG_ROWS + 24
SPARE = SIDE * SIDE * SLOT
SHOTS = 128
BOTH = 2 * SHOTS
UNROLL = 16
ORDER = (0, 1, 3, 2)
SAMPLES = 1024
TILES = SAMPLES // LANES
ODD = 256
PAIR = 128
F32 = jnp.float32
BF16 = jnp.bfloat16


def seg_index(x, y, core):
    return (x * SIDE + y) * 2 + core


def swap_pairs(step, first):
    pairs = []
    for x in range(SIDE):
        for y in range(SIDE):
            for core in range(2):
                along_x = (core == 0) == first
                to = seg_index(x ^ step, y, core) if along_x else seg_index(x, y ^ step, core)
                pairs.append((seg_index(x, y, core), to))
    return pairs


def swap(value, step, first):
    return lax.ppermute(value, "seg", swap_pairs(step, first))


def swap_cores(value):
    return lax.ppermute(value, "seg", [(i, i ^ 1) for i in range(SEGS)])


def split(value):
    high = value.astype(BF16)
    return high, (value - high.astype(F32)).astype(BF16)


def np_split(value):
    value = value.astype(np.float32)
    high = value.astype(ml_dtypes.bfloat16)
    return high, (value - high.astype(np.float32)).astype(ml_dtypes.bfloat16)


def waves(samples, bins):
    phase = np.outer(np.arange(samples), np.asarray(bins)) % SAMPLES
    angle = phase * (2.0 * math.pi / SAMPLES)
    return [np.cos(angle), -np.sin(angle)]


def time_tables():
    odd = waves(2 * ODD, 2 * np.arange(ODD) + 1)
    mid = waves(2 * PAIR, 4 * np.arange(PAIR) + 2)
    even = waves(2 * PAIR, 4 * np.arange(PAIR))
    last = np.zeros((2 * PAIR, LANES))
    last[:, 0] = 1.0 - 2.0 * (np.arange(2 * PAIR) % 2)
    blank = np.zeros((2 * PAIR, LANES))
    return [np.concatenate(t, axis=1) for t in (odd, mid, even + [last, blank])]


def patch_table():
    phase = np.outer(np.arange(PATCH), np.arange(PATCH)) % PATCH
    angle = phase * (2.0 * math.pi / PATCH)
    blocks = np.eye(SHOTS // PATCH)
    cos, sin = np.kron(blocks, np.cos(angle)), np.kron(blocks, np.sin(angle))
    return np.block([[cos, sin], [-sin, cos]])


def all_tables():
    odd, mid, even = [np_split(table) for table in time_tables()]
    forward, backward = np_split(patch_table()), np_split(patch_table().T)
    patch = np.concatenate([np.concatenate(forward), np.concatenate(backward)], axis=1)
    return np.concatenate([*odd, np.concatenate(mid, axis=1), *even, patch])


def fetch_kernel(source, rows, sems):
    copies = []
    for tile in range(TILES):
        copy = pltpu.make_async_copy(
            source.at[:, pl.ds(tile * LANES, LANES)], rows.at[pl.ds(tile * SHOTS, SHOTS)], sems.at[tile]
        )
        copy.start()
        copies.append(copy)
    for copy in copies:
        copy.wait()


ROWS = jax.ShapeDtypeStruct((SAMPLES, LANES), F32)


def fetch(source):
    return pl.pallas_call(
        fetch_kernel,
        out_shape=ROWS,
        in_specs=[pl.BlockSpec(memory_space=pltpu.HBM)],
        out_specs=pl.BlockSpec(memory_space=pltpu.VMEM),
        scratch_shapes=[pltpu.SemaphoreType.DMA((TILES,))],
        compiler_params=pltpu.CompilerParams(vmem_limit_bytes=4 << 20),
        cost_estimate=pl.CostEstimate(flops=1 << 10, bytes_accessed=1 << 20, transcendentals=0),
        name="fetch_shots",
    )(pltpu.with_memory_space_constraint(source, pltpu.HBM))


def place_kernel(first, count, base, lane, counts, spot, own, other, *refs):
    outs, (rows, acc, listed) = refs[-3 - count : -3], refs[-3:]
    low_end, high_end = first * SIDE * SLOT, (first + count) * SIDE * SLOT
    for tile in range(TILES):
        part = pl.ds(tile * SHOTS, SHOTS)
        rows[part, :] = own[part, :]
        rows[pl.ds(SAMPLES + tile * SHOTS, SHOTS), :] = other[:, pl.ds(tile * LANES, LANES)]
    acc[...] = jnp.zeros_like(acc)

    def note(shot, number):
        listed[number] = shot
        return number + counts[shot]

    number = lax.fori_loop(0, BOTH, note, 0, unroll=16)
    for i in range(UNROLL):
        listed[number + i] = BOTH
    lanes = lax.broadcasted_iota(jnp.int32, (8, LANES), 1)
    top = lax.broadcasted_iota(jnp.int32, (8, LANES), 0) == 0

    def body(n, carry):
        work = []
        for u in range(UNROLL):
            shot = listed[n * UNROLL + u]
            row = ((shot >> 7) & 1) * SAMPLES + (shot & (SHOTS - 1))
            turn = lane[shot]
            value = pltpu.roll(rows[pl.ds(row, TILES, stride=SHOTS), :], turn, 1)
            here = lanes >= turn
            next_row = pltpu.roll(jnp.where(here, 0.0, value), 1, 0)
            low = jnp.where(here, value, 0.0) + jnp.where(top, 0.0, next_row)
            start = jnp.where(shot == BOTH, high_end + 8, base[shot]) - low_end
            work.append((start, low, jnp.where(top, next_row, 0.0)))
        for start, low, high in work:
            acc[pl.ds(start, 8), :] += low
            acc[pl.ds(start + 8, 8), :] += high
        return carry

    lax.fori_loop(0, (number + UNROLL - 1) // UNROLL, body, 0)
    for k in range(count):
        for m in range(SIDE):
            slot, spots = pl.ds((k * SIDE + m) * SLOT + 8, SEG_ROWS), pl.ds(m * SEG_ROWS, SEG_ROWS)
            if ORDER[first] == 0:
                outs[k][spots, :] = acc[slot, :] + refs[1][spots, :]
            else:
                outs[k][spots, :] = acc[slot, :]
    if ORDER[first] == 0:
        mine = pl.ds(pl.multiple_of(spot[0] * SEG_ROWS, SEG_ROWS), SEG_ROWS)
        outs[0][mine, :] -= refs[0][...]


def place(first, count, base, lane, spot, own, other, *extra):
    low_end, high_end = first * SIDE * SLOT, (first + count) * SIDE * SLOT
    counts = ((base >= low_end) & (base < high_end)).astype(jnp.int32)
    smem = pl.BlockSpec(memory_space=pltpu.SMEM)
    vmem = pl.BlockSpec(memory_space=pltpu.VMEM)

    def kernel(*refs):
        place_kernel(first, count, *refs)

    return pl.pallas_call(
        kernel,
        out_shape=[jax.ShapeDtypeStruct((SIDE * SEG_ROWS, LANES), F32)] * count,
        in_specs=[smem] * 4 + [vmem] * (2 + len(extra)),
        out_specs=[vmem] * count,
        scratch_shapes=[
            pltpu.VMEM((2 * SAMPLES, LANES), F32),
            pltpu.VMEM((count * SIDE * SLOT + 32, LANES), F32),
            pltpu.SMEM((BOTH + UNROLL,), jnp.int32),
        ],
        compiler_params=pltpu.CompilerParams(vmem_limit_bytes=8 << 20),
        cost_estimate=pl.CostEstimate(flops=1 << 20, bytes_accessed=8 << 20, transcendentals=0),
        name=f"place_shots_{first}",
    )(base, lane, counts, spot, own, other, *extra)


SLOTS = jax.ShapeDtypeStruct((SPARE + 32, LANES), F32)


def aims(firing, first, second, core):
    seg, row = firing >> 15, (firing >> 7) & (SEG_ROWS - 1)
    inside = (seg & 1) == core
    kept = inside | ((row >= SEG_ROWS - 8) & (seg < SEGS - 1))
    seg = jnp.where(inside, seg, seg + 1)
    row = jnp.where(inside, row, row - SEG_ROWS)
    x, y = seg >> 3, (seg >> 1) & 3
    to_first = jnp.where(core == 0, x, y)
    to_second = jnp.where(core == 0, y, x)
    away = to_first ^ first
    slot = jnp.where(away >= 2, 5 - away, away) * SIDE + to_second
    base = jnp.where(kept, slot * SLOT + 8 + row, -1)
    base = jnp.concatenate([base, jnp.full((8,), SPARE + 8, jnp.int32)])
    return base, jnp.concatenate([firing & (LANES - 1), jnp.zeros((8,), jnp.int32)])


def times(value, high, low):
    a, b = split(value)
    both = jnp.dot(jnp.concatenate([a, b], axis=0), high[...], preferred_element_type=F32)
    return both[:SHOTS] + both[SHOTS:] + jnp.dot(a, low[...], preferred_element_type=F32)


def times_t(value, high, low):
    return split_times_t(split(value), high, low)


def split_times_t(value, high, low):
    def one(x, y):
        return lax.dot_general(x, y, (((1,), (1,)), ((), ())), preferred_element_type=F32)

    both = one(jnp.concatenate(value, axis=0), high[...])
    return both[:SHOTS] + both[SHOTS:] + one(value[0], low[...])


def mix(table, value):
    a, b = split(value)
    both = jnp.dot(table[...], a, preferred_element_type=F32)
    return both[:BOTH] + both[BOTH:] + jnp.dot(table[pl.ds(0, BOTH), :], b, preferred_element_type=F32)


def side_kernel(spot, own_base, other_base, column, residual, own_list, other_list):
    own = pl.ds(pl.multiple_of(spot[0] * SEG_ROWS, SEG_ROWS), SEG_ROWS)
    residual[...] = -column[own, :]
    for base, listed in ((own_base, own_list), (other_base, other_list)):

        def note(shot, count, base=base, listed=listed):
            listed[count] = shot
            return count + jnp.where(base[shot] >= 0, 1, 0)

        count = lax.fori_loop(0, SHOTS, note, 1, unroll=8)
        for i in range(UNROLL):
            listed[count + i] = listed[jnp.maximum(count - 1, 1)]
        listed[0] = count - 1


def side(spot, own_base, other_base, column):
    smem = pl.BlockSpec(memory_space=pltpu.SMEM)
    vmem = pl.BlockSpec(memory_space=pltpu.VMEM)
    listed = jax.ShapeDtypeStruct((SHOTS + UNROLL + 8,), jnp.int32)
    return pl.pallas_call(
        side_kernel,
        out_shape=[jax.ShapeDtypeStruct((SEG_ROWS, LANES), F32), listed, listed],
        in_specs=[smem, smem, smem, vmem],
        out_specs=[vmem, smem, smem],
        compiler_params=pltpu.CompilerParams(vmem_limit_bytes=2 << 20),
        cost_estimate=pl.CostEstimate(flops=1 << 20, bytes_accessed=8 << 20, transcendentals=0),
        name="residual_and_lists",
    )(spot, own_base, other_base, column)


def cut_windows(base, lane, listed, slots, wins):
    wins[...] = jnp.zeros_like(wins)
    lanes = lax.broadcasted_iota(jnp.int32, (8, LANES), 1)

    def body(n, carry):
        work = []
        for u in range(UNROLL):
            shot = listed[1 + n * UNROLL + u]
            start, turn = base[shot], lane[shot]
            window = jnp.where(lanes >= turn, slots[pl.ds(start, 8), :], slots[pl.ds(start + 1, 8), :])
            work.append((shot, pltpu.roll(window, (LANES - turn) & (LANES - 1), 1)))
        for shot, window in work:
            wins[pl.ds(shot, TILES, stride=SHOTS), :] = window
        return carry

    lax.fori_loop(0, (listed[0] + UNROLL - 1) // UNROLL, body, 0)


def cut_first_kernel(base, lane, listed, *refs):
    blocks, (wins, slots) = refs[:SIDE], refs[SIDE:]
    slots[pl.ds(0, 8), :] = jnp.zeros((8, LANES), F32)
    for k in range(SIDE):
        for m in range(SIDE):
            start = (ORDER.index(k) * SIDE + m) * SLOT + 8
            slots[pl.ds(start, SEG_ROWS), :] = blocks[k][pl.ds(m * SEG_ROWS, SEG_ROWS), :]
            slots[pl.ds(start + SEG_ROWS, 24), :] = jnp.zeros((24, LANES), F32)
    cut_windows(base, lane, listed, slots, wins)


WINDOWS = jax.ShapeDtypeStruct((SAMPLES, LANES), F32)


def cut_first(base, lane, listed, blocks):
    smem = pl.BlockSpec(memory_space=pltpu.SMEM)
    vmem = pl.BlockSpec(memory_space=pltpu.VMEM)
    return pl.pallas_call(
        cut_first_kernel,
        out_shape=[WINDOWS, SLOTS],
        in_specs=[smem, smem, smem] + [vmem] * SIDE,
        out_specs=[vmem, vmem],
        compiler_params=pltpu.CompilerParams(vmem_limit_bytes=8 << 20),
        cost_estimate=pl.CostEstimate(flops=1 << 20, bytes_accessed=6 << 20, transcendentals=0),
        name="cut_other_windows",
    )(base, lane, listed, *blocks)


def cut_again(base, lane, listed, slots):
    smem = pl.BlockSpec(memory_space=pltpu.SMEM)
    vmem = pl.BlockSpec(memory_space=pltpu.VMEM)
    return pl.pallas_call(
        cut_windows,
        out_shape=WINDOWS,
        in_specs=[smem, smem, smem, vmem],
        out_specs=vmem,
        compiler_params=pltpu.CompilerParams(vmem_limit_bytes=8 << 20),
        cost_estimate=pl.CostEstimate(flops=1 << 20, bytes_accessed=6 << 20, transcendentals=0),
        name="cut_own_windows",
    )(base, lane, listed, slots)


def shrink_kernel(cutoff, est, here, there, table, result, out, sems):
    tables = [
        table.at[pl.ds(0, 512), :],
        table.at[pl.ds(512, 512), :],
        table.at[pl.ds(1024, 256), pl.ds(0, 256)],
        table.at[pl.ds(1024, 256), pl.ds(256, 256)],
        table.at[pl.ds(1280, 256), pl.ds(0, 384)],
        table.at[pl.ds(1536, 256), pl.ds(0, 384)],
    ]
    fwd, bwd = table.at[pl.ds(1792, 512), pl.ds(0, 256)], table.at[pl.ds(1792, 512), pl.ds(256, 256)]
    stepped = jnp.concatenate(
        [
            est[:, pl.ds(t * LANES, LANES)] - 0.5 * (here[pl.ds(t * SHOTS, SHOTS), :] + there[pl.ds(t * SHOTS, SHOTS), :])
            for t in range(TILES)
        ],
        axis=1,
    )
    front, rear = stepped[:, :512], stepped[:, 512:]
    folded = front + rear
    odd = times(front - rear, tables[0], tables[1])
    mid = times(folded[:, :256] - folded[:, 256:], tables[2], tables[3])
    even = times(folded[:, :256] + folded[:, 256:], tables[4], tables[5])
    last = even[:, 2 * PAIR :]
    stacked = jnp.concatenate(
        [
            jnp.concatenate([odd[:, :ODD], mid[:, :PAIR], even[:, :PAIR], last], axis=1),
            jnp.concatenate(
                [odd[:, ODD:], mid[:, PAIR:], even[:, PAIR : 2 * PAIR], jnp.zeros_like(last)], axis=1
            ),
        ],
        axis=0,
    )
    coeff = mix(fwd, stacked)
    real, imag = coeff[:SHOTS], coeff[SHOTS:]
    level = cutoff[0] * 128.0
    power = real * real + imag * imag
    factor = 1.0 - level * lax.rsqrt(jnp.maximum(power, level * level))
    column = lax.broadcasted_iota(jnp.int32, real.shape, 1)
    weight = jnp.where((column == ODD + PAIR) | (column >= ODD + 2 * PAIR), 1.0, 2.0)
    factor = factor * weight * (1.0 / (PATCH * SAMPLES))
    back = mix(bwd, jnp.concatenate([real * factor, imag * factor], axis=0))
    real, imag = back[:SHOTS], back[SHOTS:]
    mid = times_t(
        jnp.concatenate([real[:, ODD : ODD + PAIR], imag[:, ODD : ODD + PAIR]], axis=1),
        tables[2],
        tables[3],
    )
    even = times_t(
        jnp.concatenate(
            [
                real[:, ODD + PAIR : ODD + 2 * PAIR],
                imag[:, ODD + PAIR : ODD + 2 * PAIR],
                real[:, ODD + 2 * PAIR :],
            ],
            axis=1,
        ),
        tables[4],
        tables[5],
    )
    spectrum = split(jnp.concatenate([real[:, :ODD], imag[:, :ODD]], axis=1))
    copies = []
    for part, front in enumerate((even + mid, even - mid)):
        spots = pl.ds(part * 2 * PAIR, 2 * PAIR)
        odd = split_times_t(spectrum, tables[0].at[spots, :], tables[1].at[spots, :])
        for sign, value in enumerate((front + odd, front - odd)):
            spots = pl.ds(sign * 512 + part * 2 * PAIR, 2 * PAIR)
            out[:, spots] = value
            copies.append(
                pltpu.make_async_copy(out.at[:, spots], result.at[:, spots], sems.at[part * 2 + sign])
            )
            copies[-1].start()
    for copy in copies:
        copy.wait()


def shrink(cutoff, est, here, there):
    vmem = pl.BlockSpec(memory_space=pltpu.VMEM)
    return pl.pallas_call(
        shrink_kernel,
        out_shape=jax.ShapeDtypeStruct((SHOTS, SAMPLES), F32),
        in_specs=[pl.BlockSpec(memory_space=pltpu.SMEM)] + [vmem] * 4,
        out_specs=pl.BlockSpec(memory_space=pl.ANY),
        scratch_shapes=[pltpu.VMEM((SHOTS, SAMPLES), F32), pltpu.SemaphoreType.DMA((4,))],
        compiler_params=pltpu.CompilerParams(vmem_limit_bytes=12 << 20),
        cost_estimate=pl.CostEstimate(flops=1 << 29, bytes_accessed=8 << 20, transcendentals=0),
        name="shrink",
    )(cutoff, est, here, there, jnp.asarray(all_tables()))


def shards(record, estimate, launch_portion, launch_offset, threshold):
    index = lax.axis_index("seg")
    core, y, x = index & 1, (index >> 1) & 3, index >> 3
    first, second = jnp.where(core == 0, x, y), jnp.where(core == 0, y, x)
    firing = launch_portion[:, 0] * (SEG_ROWS * LANES) + launch_offset
    record = record.reshape(SEG_ROWS, LANES)
    spot = second.reshape(1)

    other = swap_cores(estimate)
    other_firing = swap_cores(launch_portion)[:, 0] * (SEG_ROWS * LANES) + swap_cores(launch_offset)
    own_aims = aims(firing, first, second, core)
    other_aims = aims(other_firing, first, second, core)
    base, lane = [jnp.concatenate([a[:SHOTS], b]) for a, b in zip(own_aims, other_aims)]
    shots = (base, lane, spot, fetch(estimate), other)

    (opposite,) = place(3, 1, *shots)
    opposite = swap(opposite, 2, True)
    one, three = place(1, 2, *shots)
    (column,) = place(0, 1, *shots, record, opposite)
    column = column + swap(one, 1, True) + swap(three, 3, True)
    arrived = [swap(column, k, False) for k in (2, 1, 3)]
    column = column + arrived[0] + arrived[1] + arrived[2]

    residual, own_list, other_list = side(spot, own_aims[0], other_aims[0], column)
    far_blocks = {k: swap(column, k, True) for k in (2, 1, 3)}

    far_blocks[0] = column
    blocks = [far_blocks[k] for k in range(SIDE)]
    windows, slots = cut_first(*other_aims, other_list, blocks)
    there = swap_cores(windows)
    here = cut_again(*own_aims, own_list, slots)
    updated = shrink(threshold, estimate, here, there)
    return (updated, residual.reshape(-1))


def solution(mesh):
    placed = (P(("node", "seg")), P(("node", "seg"), None), P("seg", None), P("seg"), P())
    return jax.shard_map(
        shards,
        mesh=mesh,
        in_specs=placed,
        out_specs=(P(("node", "seg"), None), P(("node", "seg"))),
        check_vma=False,
    )
```

```python
import math

import jax
import jax.numpy as jnp
import ml_dtypes
import numpy as np
from jax import lax
from jax.experimental import pallas as pl
from jax.experimental.pallas import tpu as pltpu
from jax.sharding import PartitionSpec as P

PATCH = 16
LANES = 128
SIDE = 4
SEGS = 32
SEG_ROWS = 256
SLOT = SEG_ROWS + 24
SPARE = SIDE * SIDE * SLOT
SHOTS = 128
BOTH = 2 * SHOTS
UNROLL = 16
ORDER = (0, 1, 3, 2)
SAMPLES = 1024
TILES = SAMPLES // LANES
ODD = 256
PAIR = 128
F32 = jnp.float32
BF16 = jnp.bfloat16


def seg_index(x, y, core):
    return (x * SIDE + y) * 2 + core


def swap_pairs(step, first):
    pairs = []
    for x in range(SIDE):
        for y in range(SIDE):
            for core in range(2):
                along_x = (core == 0) == first
                to = seg_index(x ^ step, y, core) if along_x else seg_index(x, y ^ step, core)
                pairs.append((seg_index(x, y, core), to))
    return pairs


def swap(value, step, first):
    return lax.ppermute(value, "seg", swap_pairs(step, first))


def swap_cores(value):
    return lax.ppermute(value, "seg", [(i, i ^ 1) for i in range(SEGS)])


def split(value):
    high = value.astype(BF16)
    return high, (value - high.astype(F32)).astype(BF16)


def np_split(value):
    value = value.astype(np.float32)
    high = value.astype(ml_dtypes.bfloat16)
    return high, (value - high.astype(np.float32)).astype(ml_dtypes.bfloat16)


def waves(samples, bins):
    phase = np.outer(np.arange(samples), np.asarray(bins)) % SAMPLES
    angle = phase * (2.0 * math.pi / SAMPLES)
    return [np.cos(angle), -np.sin(angle)]


def time_tables():
    odd = waves(2 * ODD, 2 * np.arange(ODD) + 1)
    mid = waves(2 * PAIR, 4 * np.arange(PAIR) + 2)
    even = waves(2 * PAIR, 4 * np.arange(PAIR))
    last = np.zeros((2 * PAIR, LANES))
    last[:, 0] = 1.0 - 2.0 * (np.arange(2 * PAIR) % 2)
    blank = np.zeros((2 * PAIR, LANES))
    return [np.concatenate(t, axis=1) for t in (odd, mid, even + [last, blank])]


def patch_table():
    phase = np.outer(np.arange(PATCH), np.arange(PATCH)) % PATCH
    angle = phase * (2.0 * math.pi / PATCH)
    blocks = np.eye(SHOTS // PATCH)
    cos, sin = np.kron(blocks, np.cos(angle)), np.kron(blocks, np.sin(angle))
    return np.block([[cos, sin], [-sin, cos]])


def all_tables():
    odd, mid, even = [np_split(table) for table in time_tables()]
    forward, backward = np_split(patch_table()), np_split(patch_table().T)
    patch = np.concatenate([np.concatenate(forward), np.concatenate(backward)], axis=1)
    return np.concatenate([*odd, np.concatenate(mid, axis=1), *even, patch])


def fetch_kernel(source, portion, offset, rows, portion_out, offset_out, sems):
    copies = [(portion, portion_out), (offset, offset_out)]
    for tile in range(TILES):
        copies.append((source.at[:, pl.ds(tile * LANES, LANES)], rows.at[pl.ds(tile * SHOTS, SHOTS)]))
    copies = [pltpu.make_async_copy(*pair, sems.at[i]) for i, pair in enumerate(copies)]
    for copy in copies:
        copy.start()
    for copy in copies:
        copy.wait()


ROWS = jax.ShapeDtypeStruct((SAMPLES, LANES), F32)


def fetch(source, portion, offset):
    inputs = [pltpu.with_memory_space_constraint(x, pltpu.HBM) for x in (source, portion, offset)]
    whens = jax.ShapeDtypeStruct((1, SHOTS), jnp.int32)
    rows, portion, offset = pl.pallas_call(
        fetch_kernel,
        out_shape=[ROWS, whens, whens],
        in_specs=[pl.BlockSpec(memory_space=pltpu.HBM)] * 3,
        out_specs=[pl.BlockSpec(memory_space=pltpu.VMEM)] * 3,
        scratch_shapes=[pltpu.SemaphoreType.DMA((TILES + 2,))],
        compiler_params=pltpu.CompilerParams(vmem_limit_bytes=4 << 20),
        cost_estimate=pl.CostEstimate(flops=1 << 10, bytes_accessed=1 << 20, transcendentals=0),
        name="fetch_shots",
    )(*inputs)
    return rows, portion[0] * (SEG_ROWS * LANES) + offset[0]


def place_kernel(first, count, other, own, base, lane, counts, spot, *refs):
    outs, (rows, acc, listed) = refs[-3 - count : -3], refs[-3:]
    low_end, high_end = first * SIDE * SLOT, (first + count) * SIDE * SLOT
    for tile in range(TILES):
        part = pl.ds(tile * SHOTS, SHOTS)
        rows[part, :] = own[part, :]
        rows[pl.ds(SAMPLES + tile * SHOTS, SHOTS), :] = other[:, pl.ds(tile * LANES, LANES)]
    acc[...] = jnp.zeros_like(acc)

    def note(shot, number):
        listed[number] = shot
        return number + counts[shot]

    number = lax.fori_loop(0, BOTH, note, 0, unroll=16)
    for i in range(UNROLL):
        listed[number + i] = BOTH
    lanes = lax.broadcasted_iota(jnp.int32, (8, LANES), 1)
    top = lax.broadcasted_iota(jnp.int32, (8, LANES), 0) == 0

    def body(n, carry):
        work = []
        for u in range(UNROLL):
            shot = listed[n * UNROLL + u]
            row = ((shot >> 7) & 1) * SAMPLES + (shot & (SHOTS - 1))
            turn = lane[shot]
            value = pltpu.roll(rows[pl.ds(row, TILES, stride=SHOTS), :], turn, 1)
            here = lanes >= turn
            next_row = pltpu.roll(jnp.where(here, 0.0, value), 1, 0)
            low = jnp.where(here, value, 0.0) + jnp.where(top, 0.0, next_row)
            start = jnp.where(shot == BOTH, high_end + 8, base[shot]) - low_end
            work.append((start, low, jnp.where(top, next_row, 0.0)))
        for start, low, high in work:
            acc[pl.ds(start, 8), :] += low
            acc[pl.ds(start + 8, 8), :] += high
        return carry

    lax.fori_loop(0, (number + UNROLL - 1) // UNROLL, body, 0)
    for k in range(count):
        for m in range(SIDE):
            slot, spots = pl.ds((k * SIDE + m) * SLOT + 8, SEG_ROWS), pl.ds(m * SEG_ROWS, SEG_ROWS)
            if ORDER[first] == 0:
                outs[k][spots, :] = acc[slot, :] + refs[1][spots, :]
            else:
                outs[k][spots, :] = acc[slot, :]
    if ORDER[first] == 0:
        mine = pl.ds(pl.multiple_of(spot[0] * SEG_ROWS, SEG_ROWS), SEG_ROWS)
        outs[0][mine, :] -= refs[0][...]


def place(first, count, base, lane, spot, own, other, *extra):
    low_end, high_end = first * SIDE * SLOT, (first + count) * SIDE * SLOT
    counts = ((base >= low_end) & (base < high_end)).astype(jnp.int32)
    smem = pl.BlockSpec(memory_space=pltpu.SMEM)
    vmem = pl.BlockSpec(memory_space=pltpu.VMEM)

    def kernel(*refs):
        place_kernel(first, count, *refs)

    return pl.pallas_call(
        kernel,
        out_shape=[jax.ShapeDtypeStruct((SIDE * SEG_ROWS, LANES), F32)] * count,
        in_specs=[vmem] * 2 + [smem] * 4 + [vmem] * len(extra),
        out_specs=[vmem] * count,
        scratch_shapes=[
            pltpu.VMEM((2 * SAMPLES, LANES), F32),
            pltpu.VMEM((count * SIDE * SLOT + 32, LANES), F32),
            pltpu.SMEM((BOTH + UNROLL,), jnp.int32),
        ],
        compiler_params=pltpu.CompilerParams(vmem_limit_bytes=8 << 20),
        cost_estimate=pl.CostEstimate(flops=1 << 20, bytes_accessed=8 << 20, transcendentals=0),
        name=f"place_shots_{first}",
    )(other, own, base, lane, counts, spot, *extra)


SLOTS = jax.ShapeDtypeStruct((SPARE + 32, LANES), F32)


def aims(firing, first, second, core):
    seg, row = firing >> 15, (firing >> 7) & (SEG_ROWS - 1)
    inside = (seg & 1) == core
    kept = inside | ((row >= SEG_ROWS - 8) & (seg < SEGS - 1))
    seg = jnp.where(inside, seg, seg + 1)
    row = jnp.where(inside, row, row - SEG_ROWS)
    x, y = seg >> 3, (seg >> 1) & 3
    to_first = jnp.where(core == 0, x, y)
    to_second = jnp.where(core == 0, y, x)
    away = to_first ^ first
    slot = jnp.where(away >= 2, 5 - away, away) * SIDE + to_second
    base = jnp.where(kept, slot * SLOT + 8 + row, -1)
    base = jnp.concatenate([base, jnp.full((8,), SPARE + 8, jnp.int32)])
    return base, jnp.concatenate([firing & (LANES - 1), jnp.zeros((8,), jnp.int32)])


def times(value, high, low):
    a, b = split(value)
    both = jnp.dot(jnp.concatenate([a, b], axis=0), high[...], preferred_element_type=F32)
    return both[:SHOTS] + both[SHOTS:] + jnp.dot(a, low[...], preferred_element_type=F32)


def times_t(value, high, low):
    return split_times_t(split(value), high, low)


def split_times_t(value, high, low):
    def one(x, y):
        return lax.dot_general(x, y, (((1,), (1,)), ((), ())), preferred_element_type=F32)

    both = one(jnp.concatenate(value, axis=0), high[...])
    return both[:SHOTS] + both[SHOTS:] + one(value[0], low[...])


def mix(table, value):
    a, b = split(value)
    both = jnp.dot(table[...], a, preferred_element_type=F32)
    return both[:BOTH] + both[BOTH:] + jnp.dot(table[pl.ds(0, BOTH), :], b, preferred_element_type=F32)


EARLY, LATE = (0, 2), (1, 3)


def side_kernel(column, spot, *refs):
    count = (len(refs) - 1) // 2
    flags, residual, lists = refs[:count], refs[count], refs[count + 1 :]
    own = pl.ds(pl.multiple_of(spot[0] * SEG_ROWS, SEG_ROWS), SEG_ROWS)
    residual[...] = -column[own, :]
    for flag, listed in zip(flags, lists):

        def note(shot, count, flag=flag, listed=listed):
            listed[count] = shot
            return count + flag[shot]

        count = lax.fori_loop(0, SHOTS, note, 1, unroll=8)
        for i in range(UNROLL):
            listed[count + i] = listed[jnp.maximum(count - 1, 1)]
        listed[0] = count - 1


def side(spot, bases, column):
    smem = pl.BlockSpec(memory_space=pltpu.SMEM)
    vmem = pl.BlockSpec(memory_space=pltpu.VMEM)
    listed = jax.ShapeDtypeStruct((SHOTS + UNROLL + 8,), jnp.int32)
    flags = []
    for base in bases:
        late = (base >= SIDE * SLOT) & (base < 3 * SIDE * SLOT)
        flags += [((base >= 0) & ~late).astype(jnp.int32), late.astype(jnp.int32)]
    return pl.pallas_call(
        side_kernel,
        out_shape=[jax.ShapeDtypeStruct((SEG_ROWS, LANES), F32)] + [listed] * len(flags),
        in_specs=[vmem] + [smem] * (1 + len(flags)),
        out_specs=[vmem] + [smem] * len(flags),
        compiler_params=pltpu.CompilerParams(vmem_limit_bytes=2 << 20),
        cost_estimate=pl.CostEstimate(flops=1 << 20, bytes_accessed=8 << 20, transcendentals=0),
        name="residual_and_lists",
    )(column, spot, *flags)


def fill_slots(columns, blocks, slots):
    for k, block in zip(columns, blocks):
        for m in range(SIDE):
            start = (ORDER.index(k) * SIDE + m) * SLOT
            slots[pl.ds(start, 8), :] = jnp.zeros((8, LANES), F32)
            slots[pl.ds(start + 8, SEG_ROWS), :] = block[pl.ds(m * SEG_ROWS, SEG_ROWS), :]
            slots[pl.ds(start + 8 + SEG_ROWS, 16), :] = jnp.zeros((16, LANES), F32)


def cut_windows(base, lane, listed, slots, wins):
    lanes = lax.broadcasted_iota(jnp.int32, (8, LANES), 1)

    def body(n, carry):
        work = []
        for u in range(UNROLL):
            shot = listed[1 + n * UNROLL + u]
            start, turn = base[shot], lane[shot]
            window = jnp.where(lanes >= turn, slots[pl.ds(start, 8), :], slots[pl.ds(start + 1, 8), :])
            work.append((shot, pltpu.roll(window, (LANES - turn) & (LANES - 1), 1)))
        for shot, window in work:
            wins[pl.ds(shot, TILES, stride=SHOTS), :] = window
        return carry

    lax.fori_loop(0, (listed[0] + UNROLL - 1) // UNROLL, body, 0)


def cut_early_kernel(*refs):
    aims, blocks, (other, own, slots) = refs[:6], refs[6:8], refs[8:]
    fill_slots(EARLY, blocks, slots)
    for i, wins in enumerate((other, own)):
        wins[...] = jnp.zeros_like(wins)
        cut_windows(*aims[3 * i : 3 * i + 3], slots, wins)


def cut_other_kernel(base, lane, listed, early, *refs):
    blocks, (wins, slots) = refs[:2], refs[2:]
    fill_slots(LATE, blocks, slots)
    wins[...] = early[...]
    cut_windows(base, lane, listed, slots, wins)


def cut_own_kernel(base, lane, listed, early, slots, wins):
    wins[...] = early[...]
    cut_windows(base, lane, listed, slots, wins)


WINDOWS = jax.ShapeDtypeStruct((SAMPLES, LANES), F32)


def cut(kernel, aims, arrays, out_shape, scratch=()):
    smem = pl.BlockSpec(memory_space=pltpu.SMEM)
    vmem = pl.BlockSpec(memory_space=pltpu.VMEM)
    return pl.pallas_call(
        kernel,
        out_shape=out_shape,
        in_specs=[smem] * len(aims) + [vmem] * len(arrays),
        out_specs=[vmem] * len(out_shape),
        scratch_shapes=scratch,
        compiler_params=pltpu.CompilerParams(vmem_limit_bytes=8 << 20),
        cost_estimate=pl.CostEstimate(flops=1 << 20, bytes_accessed=6 << 20, transcendentals=0),
        name=kernel.__name__,
    )(*aims, *arrays)


def shrink_kernel(cutoff, est, here, there, table, result, out, sems):
    tables = [
        table.at[pl.ds(0, 512), :],
        table.at[pl.ds(512, 512), :],
        table.at[pl.ds(1024, 256), pl.ds(0, 256)],
        table.at[pl.ds(1024, 256), pl.ds(256, 256)],
        table.at[pl.ds(1280, 256), pl.ds(0, 384)],
        table.at[pl.ds(1536, 256), pl.ds(0, 384)],
    ]
    fwd, bwd = table.at[pl.ds(1792, 512), pl.ds(0, 256)], table.at[pl.ds(1792, 512), pl.ds(256, 256)]
    stepped = jnp.concatenate(
        [
            est[:, pl.ds(t * LANES, LANES)] - 0.5 * (here[pl.ds(t * SHOTS, SHOTS), :] + there[pl.ds(t * SHOTS, SHOTS), :])
            for t in range(TILES)
        ],
        axis=1,
    )
    front, rear = stepped[:, :512], stepped[:, 512:]
    folded = front + rear
    odd = times(front - rear, tables[0], tables[1])
    mid = times(folded[:, :256] - folded[:, 256:], tables[2], tables[3])
    even = times(folded[:, :256] + folded[:, 256:], tables[4], tables[5])
    last = even[:, 2 * PAIR :]
    stacked = jnp.concatenate(
        [
            jnp.concatenate([odd[:, :ODD], mid[:, :PAIR], even[:, :PAIR], last], axis=1),
            jnp.concatenate(
                [odd[:, ODD:], mid[:, PAIR:], even[:, PAIR : 2 * PAIR], jnp.zeros_like(last)], axis=1
            ),
        ],
        axis=0,
    )
    coeff = mix(fwd, stacked)
    real, imag = coeff[:SHOTS], coeff[SHOTS:]
    level = cutoff[0] * 128.0
    power = real * real + imag * imag
    factor = 1.0 - level * lax.rsqrt(jnp.maximum(power, level * level))
    column = lax.broadcasted_iota(jnp.int32, real.shape, 1)
    weight = jnp.where((column == ODD + PAIR) | (column >= ODD + 2 * PAIR), 1.0, 2.0)
    factor = factor * weight * (1.0 / (PATCH * SAMPLES))
    back = mix(bwd, jnp.concatenate([real * factor, imag * factor], axis=0))
    real, imag = back[:SHOTS], back[SHOTS:]
    mid = times_t(
        jnp.concatenate([real[:, ODD : ODD + PAIR], imag[:, ODD : ODD + PAIR]], axis=1),
        tables[2],
        tables[3],
    )
    even = times_t(
        jnp.concatenate(
            [
                real[:, ODD + PAIR : ODD + 2 * PAIR],
                imag[:, ODD + PAIR : ODD + 2 * PAIR],
                real[:, ODD + 2 * PAIR :],
            ],
            axis=1,
        ),
        tables[4],
        tables[5],
    )
    spectrum = split(jnp.concatenate([real[:, :ODD], imag[:, :ODD]], axis=1))
    copies = []
    for part, front in enumerate((even + mid, even - mid)):
        spots = pl.ds(part * 2 * PAIR, 2 * PAIR)
        odd = split_times_t(spectrum, tables[0].at[spots, :], tables[1].at[spots, :])
        for sign, value in enumerate((front + odd, front - odd)):
            spots = pl.ds(sign * 512 + part * 2 * PAIR, 2 * PAIR)
            out[:, spots] = value
            copies.append(
                pltpu.make_async_copy(out.at[:, spots], result.at[:, spots], sems.at[part * 2 + sign])
            )
            copies[-1].start()
    for copy in copies:
        copy.wait()


def shrink(cutoff, est, here, there):
    vmem = pl.BlockSpec(memory_space=pltpu.VMEM)
    return pl.pallas_call(
        shrink_kernel,
        out_shape=jax.ShapeDtypeStruct((SHOTS, SAMPLES), F32),
        in_specs=[pl.BlockSpec(memory_space=pltpu.SMEM)] + [vmem] * 4,
        out_specs=pl.BlockSpec(memory_space=pl.ANY),
        scratch_shapes=[pltpu.VMEM((SHOTS, SAMPLES), F32), pltpu.SemaphoreType.DMA((4,))],
        compiler_params=pltpu.CompilerParams(vmem_limit_bytes=12 << 20),
        cost_estimate=pl.CostEstimate(flops=1 << 29, bytes_accessed=8 << 20, transcendentals=0),
        name="shrink",
    )(cutoff, est, here, there, jnp.asarray(all_tables()))


def shards(record, estimate, launch_portion, launch_offset, threshold):
    index = lax.axis_index("seg")
    core, y, x = index & 1, (index >> 1) & 3, index >> 3
    first, second = jnp.where(core == 0, x, y), jnp.where(core == 0, y, x)
    record = record.reshape(SEG_ROWS, LANES)
    spot = second.reshape(1)

    other = swap_cores(estimate)
    rows, firing = fetch(estimate, launch_portion.reshape(1, SHOTS), launch_offset.reshape(1, SHOTS))
    other_firing = swap_cores(launch_portion)[:, 0] * (SEG_ROWS * LANES) + swap_cores(launch_offset)
    own_aims = aims(firing, first, second, core)
    other_aims = aims(other_firing, first, second, core)
    base, lane = [jnp.concatenate([a[:SHOTS], b]) for a, b in zip(own_aims, other_aims)]
    shots = (base, lane, spot, rows, other)

    (opposite,) = place(3, 1, *shots)
    opposite = swap(opposite, 2, True)
    one, three = place(1, 2, *shots)
    (column,) = place(0, 1, *shots, record, opposite)
    column = column + swap(one, 1, True) + swap(three, 3, True)
    arrived = [swap(column, k, False) for k in (2, 1, 3)]
    column = column + arrived[0] + arrived[1] + arrived[2]

    residual, *lists = side(spot, (other_aims[0], own_aims[0]), column)
    far_blocks = {k: swap(column, k, True) for k in (2, 1, 3)}

    far_blocks[0] = column

    others, owns = cut(
        cut_early_kernel,
        (*other_aims, lists[0], *own_aims, lists[2]),
        [far_blocks[k] for k in EARLY],
        [WINDOWS] * 2,
        [pltpu.VMEM(SLOTS.shape, F32)],
    )
    late = [far_blocks[k] for k in LATE]
    others, slots = cut(cut_other_kernel, (*other_aims, lists[1]), [others, *late], [WINDOWS, SLOTS])
    there = swap_cores(others)
    (here,) = cut(cut_own_kernel, (*own_aims, lists[3]), [owns, slots], [WINDOWS])
    updated = shrink(threshold, estimate, here, there)
    return (updated, residual.reshape(-1))


def solution(mesh):
    placed = (P(("node", "seg")), P(("node", "seg"), None), P("seg", None), P("seg"), P())
    return jax.shard_map(
        shards,
        mesh=mesh,
        in_specs=placed,
        out_specs=(P(("node", "seg"), None), P(("node", "seg"))),
        check_vma=False,
    )
```

```python
import math

import jax
import jax.numpy as jnp
import ml_dtypes
import numpy as np
from jax import lax
from jax.experimental import pallas as pl
from jax.experimental.pallas import tpu as pltpu
from jax.sharding import PartitionSpec as P

PATCH = 16
LANES = 128
SIDE = 4
SEGS = 32
SEG_ROWS = 256
SLOT = SEG_ROWS + 24
SPARE = SIDE * SIDE * SLOT
SHOTS = 128
BOTH = 2 * SHOTS
UNROLL = 16
ORDER = (0, 1, 3, 2)
SAMPLES = 1024
TILES = SAMPLES // LANES
ODD = 256
PAIR = 128
F32 = jnp.float32
BF16 = jnp.bfloat16


def seg_index(x, y, core):
    return (x * SIDE + y) * 2 + core


def swap_pairs(step, first):
    pairs = []
    for x in range(SIDE):
        for y in range(SIDE):
            for core in range(2):
                along_x = (core == 0) == first
                to = seg_index(x ^ step, y, core) if along_x else seg_index(x, y ^ step, core)
                pairs.append((seg_index(x, y, core), to))
    return pairs


def swap(value, step, first):
    return lax.ppermute(value, "seg", swap_pairs(step, first))


def swap_cores(value):
    return lax.ppermute(value, "seg", [(i, i ^ 1) for i in range(SEGS)])


def split(value):
    high = value.astype(BF16)
    return high, (value - high.astype(F32)).astype(BF16)


def np_split(value):
    value = value.astype(np.float32)
    high = value.astype(ml_dtypes.bfloat16)
    return high, (value - high.astype(np.float32)).astype(ml_dtypes.bfloat16)


def waves(samples, bins):
    phase = np.outer(np.arange(samples), np.asarray(bins)) % SAMPLES
    angle = phase * (2.0 * math.pi / SAMPLES)
    return [np.cos(angle), -np.sin(angle)]


def time_tables():
    odd = waves(2 * ODD, 2 * np.arange(ODD) + 1)
    mid = waves(2 * PAIR, 4 * np.arange(PAIR) + 2)
    even = waves(2 * PAIR, 4 * np.arange(PAIR))
    last = np.zeros((2 * PAIR, LANES))
    last[:, 0] = 1.0 - 2.0 * (np.arange(2 * PAIR) % 2)
    blank = np.zeros((2 * PAIR, LANES))
    return [np.concatenate(t, axis=1) for t in (odd, mid, even + [last, blank])]


def patch_table():
    phase = np.outer(np.arange(PATCH), np.arange(PATCH)) % PATCH
    angle = phase * (2.0 * math.pi / PATCH)
    blocks = np.eye(SHOTS // PATCH)
    cos, sin = np.kron(blocks, np.cos(angle)), np.kron(blocks, np.sin(angle))
    return np.block([[cos, sin], [-sin, cos]])


def all_tables():
    odd, mid, even = [np_split(table) for table in time_tables()]
    forward, backward = np_split(patch_table()), np_split(patch_table().T)
    patch = np.concatenate([np.concatenate(forward), np.concatenate(backward)], axis=1)
    return np.concatenate([*odd, np.concatenate(mid, axis=1), *even, patch])


def fetch_kernel(source, portion, offset, rows, portion_out, offset_out, sems):
    copies = [(portion, portion_out), (offset, offset_out)]
    for tile in range(TILES):
        copies.append((source.at[:, pl.ds(tile * LANES, LANES)], rows.at[pl.ds(tile * SHOTS, SHOTS)]))
    copies = [pltpu.make_async_copy(*pair, sems.at[i]) for i, pair in enumerate(copies)]
    for copy in copies:
        copy.start()
    for copy in copies:
        copy.wait()


ROWS = jax.ShapeDtypeStruct((SAMPLES, LANES), F32)


def fetch(source, portion, offset):
    inputs = [pltpu.with_memory_space_constraint(x, pltpu.HBM) for x in (source, portion, offset)]
    whens = jax.ShapeDtypeStruct((1, SHOTS), jnp.int32)
    rows, portion, offset = pl.pallas_call(
        fetch_kernel,
        out_shape=[ROWS, whens, whens],
        in_specs=[pl.BlockSpec(memory_space=pltpu.HBM)] * 3,
        out_specs=[pl.BlockSpec(memory_space=pltpu.VMEM)] * 3,
        scratch_shapes=[pltpu.SemaphoreType.DMA((TILES + 2,))],
        compiler_params=pltpu.CompilerParams(vmem_limit_bytes=4 << 20),
        cost_estimate=pl.CostEstimate(flops=1 << 10, bytes_accessed=1 << 20, transcendentals=0),
        name="fetch_shots",
    )(*inputs)
    return rows, portion[0] * (SEG_ROWS * LANES) + offset[0]


def join_kernel(other, own, rows):
    rows[pl.ds(0, SAMPLES), :] = own[...]
    for tile in range(TILES):
        rows[pl.ds(SAMPLES + tile * SHOTS, SHOTS), :] = other[:, pl.ds(tile * LANES, LANES)]


def join(other, own):
    vmem = pl.BlockSpec(memory_space=pltpu.VMEM)
    return pl.pallas_call(
        join_kernel,
        out_shape=jax.ShapeDtypeStruct((2 * SAMPLES, LANES), F32),
        in_specs=[vmem] * 2,
        out_specs=vmem,
        compiler_params=pltpu.CompilerParams(vmem_limit_bytes=4 << 20),
        cost_estimate=pl.CostEstimate(flops=1, bytes_accessed=1, transcendentals=0),
        name="join_shots",
    )(other, own)


def place_kernel(first, count, rows, base, lane, counts, spot, *refs):
    outs, (acc, listed) = refs[-2 - count : -2], refs[-2:]
    low_end, high_end = first * SIDE * SLOT, (first + count) * SIDE * SLOT
    acc[...] = jnp.zeros_like(acc)

    def note(shot, number):
        listed[number] = shot
        return number + counts[shot]

    number = lax.fori_loop(0, BOTH, note, 0, unroll=16)
    for i in range(UNROLL):
        listed[number + i] = BOTH
    lanes = lax.broadcasted_iota(jnp.int32, (8, LANES), 1)
    top = lax.broadcasted_iota(jnp.int32, (8, LANES), 0) == 0

    def body(n, carry):
        work = []
        for u in range(UNROLL):
            shot = listed[n * UNROLL + u]
            row = ((shot >> 7) & 1) * SAMPLES + (shot & (SHOTS - 1))
            turn = lane[shot]
            value = pltpu.roll(rows[pl.ds(row, TILES, stride=SHOTS), :], turn, 1)
            here = lanes >= turn
            next_row = pltpu.roll(jnp.where(here, 0.0, value), 1, 0)
            low = jnp.where(here, value, 0.0) + jnp.where(top, 0.0, next_row)
            start = jnp.where(shot == BOTH, high_end + 8, base[shot]) - low_end
            work.append((start, low, jnp.where(top, next_row, 0.0)))
        for start, low, high in work:
            acc[pl.ds(start, 8), :] += low
            acc[pl.ds(start + 8, 8), :] += high
        return carry

    lax.fori_loop(0, (number + UNROLL - 1) // UNROLL, body, 0)
    for k in range(count):
        for m in range(SIDE):
            slot, spots = pl.ds((k * SIDE + m) * SLOT + 8, SEG_ROWS), pl.ds(m * SEG_ROWS, SEG_ROWS)
            if ORDER[first] == 0:
                outs[k][spots, :] = acc[slot, :] + refs[1][spots, :]
            else:
                outs[k][spots, :] = acc[slot, :]
    if ORDER[first] == 0:
        mine = pl.ds(pl.multiple_of(spot[0] * SEG_ROWS, SEG_ROWS), SEG_ROWS)
        outs[0][mine, :] -= refs[0][...]


def place(first, count, base, lane, spot, rows, *extra):
    low_end, high_end = first * SIDE * SLOT, (first + count) * SIDE * SLOT
    counts = ((base >= low_end) & (base < high_end)).astype(jnp.int32)
    smem = pl.BlockSpec(memory_space=pltpu.SMEM)
    vmem = pl.BlockSpec(memory_space=pltpu.VMEM)

    def kernel(*refs):
        place_kernel(first, count, *refs)

    return pl.pallas_call(
        kernel,
        out_shape=[jax.ShapeDtypeStruct((SIDE * SEG_ROWS, LANES), F32)] * count,
        in_specs=[vmem] + [smem] * 4 + [vmem] * len(extra),
        out_specs=[vmem] * count,
        scratch_shapes=[
            pltpu.VMEM((count * SIDE * SLOT + 32, LANES), F32),
            pltpu.SMEM((BOTH + UNROLL,), jnp.int32),
        ],
        compiler_params=pltpu.CompilerParams(vmem_limit_bytes=8 << 20),
        cost_estimate=pl.CostEstimate(flops=1 << 20, bytes_accessed=8 << 20, transcendentals=0),
        name=f"place_shots_{first}",
    )(rows, base, lane, counts, spot, *extra)


SLOTS = jax.ShapeDtypeStruct((SPARE + 32, LANES), F32)


def aims(firing, first, second, core):
    seg, row = firing >> 15, (firing >> 7) & (SEG_ROWS - 1)
    inside = (seg & 1) == core
    kept = inside | ((row >= SEG_ROWS - 8) & (seg < SEGS - 1))
    seg = jnp.where(inside, seg, seg + 1)
    row = jnp.where(inside, row, row - SEG_ROWS)
    x, y = seg >> 3, (seg >> 1) & 3
    to_first = jnp.where(core == 0, x, y)
    to_second = jnp.where(core == 0, y, x)
    away = to_first ^ first
    slot = jnp.where(away >= 2, 5 - away, away) * SIDE + to_second
    base = jnp.where(kept, slot * SLOT + 8 + row, -1)
    base = jnp.concatenate([base, jnp.full((8,), SPARE + 8, jnp.int32)])
    return base, jnp.concatenate([firing & (LANES - 1), jnp.zeros((8,), jnp.int32)])


def times(value, high, low):
    a, b = split(value)
    both = jnp.dot(jnp.concatenate([a, b], axis=0), high[...], preferred_element_type=F32)
    return both[:SHOTS] + both[SHOTS:] + jnp.dot(a, low[...], preferred_element_type=F32)


def times_t(value, high, low):
    return split_times_t(split(value), high, low)


def split_times_t(value, high, low):
    def one(x, y):
        return lax.dot_general(x, y, (((1,), (1,)), ((), ())), preferred_element_type=F32)

    both = one(jnp.concatenate(value, axis=0), high[...])
    return both[:SHOTS] + both[SHOTS:] + one(value[0], low[...])


def mix(table, value):
    a, b = split(value)
    both = jnp.dot(table[...], a, preferred_element_type=F32)
    return both[:BOTH] + both[BOTH:] + jnp.dot(table[pl.ds(0, BOTH), :], b, preferred_element_type=F32)


EARLY, LATE = (0, 2), (1, 3)


def side_kernel(column, spot, *refs):
    count = (len(refs) - 1) // 2
    flags, residual, lists = refs[:count], refs[count], refs[count + 1 :]
    own = pl.ds(pl.multiple_of(spot[0] * SEG_ROWS, SEG_ROWS), SEG_ROWS)
    residual[...] = -column[own, :]
    for flag, listed in zip(flags, lists):

        def note(shot, count, flag=flag, listed=listed):
            listed[count] = shot
            return count + flag[shot]

        count = lax.fori_loop(0, SHOTS, note, 1, unroll=8)
        for i in range(UNROLL):
            listed[count + i] = listed[jnp.maximum(count - 1, 1)]
        listed[0] = count - 1


def side(spot, bases, column):
    smem = pl.BlockSpec(memory_space=pltpu.SMEM)
    vmem = pl.BlockSpec(memory_space=pltpu.VMEM)
    listed = jax.ShapeDtypeStruct((SHOTS + UNROLL + 8,), jnp.int32)
    flags = []
    for base in bases:
        late = (base >= SIDE * SLOT) & (base < 3 * SIDE * SLOT)
        flags += [((base >= 0) & ~late).astype(jnp.int32), late.astype(jnp.int32)]
    return pl.pallas_call(
        side_kernel,
        out_shape=[jax.ShapeDtypeStruct((SEG_ROWS, LANES), F32)] + [listed] * len(flags),
        in_specs=[vmem] + [smem] * (1 + len(flags)),
        out_specs=[vmem] + [smem] * len(flags),
        compiler_params=pltpu.CompilerParams(vmem_limit_bytes=2 << 20),
        cost_estimate=pl.CostEstimate(flops=1 << 20, bytes_accessed=8 << 20, transcendentals=0),
        name="residual_and_lists",
    )(column, spot, *flags)


def fill_slots(columns, blocks, slots):
    for k, block in zip(columns, blocks):
        for m in range(SIDE):
            start = (ORDER.index(k) * SIDE + m) * SLOT
            slots[pl.ds(start, 8), :] = jnp.zeros((8, LANES), F32)
            slots[pl.ds(start + 8, SEG_ROWS), :] = block[pl.ds(m * SEG_ROWS, SEG_ROWS), :]
            slots[pl.ds(start + 8 + SEG_ROWS, 16), :] = jnp.zeros((16, LANES), F32)


def cut_windows(base, lane, listed, slots, wins):
    lanes = lax.broadcasted_iota(jnp.int32, (8, LANES), 1)

    def body(n, carry):
        work = []
        for u in range(UNROLL):
            shot = listed[1 + n * UNROLL + u]
            start, turn = base[shot], lane[shot]
            window = jnp.where(lanes >= turn, slots[pl.ds(start, 8), :], slots[pl.ds(start + 1, 8), :])
            work.append((shot, pltpu.roll(window, (LANES - turn) & (LANES - 1), 1)))
        for shot, window in work:
            wins[pl.ds(shot, TILES, stride=SHOTS), :] = window
        return carry

    lax.fori_loop(0, (listed[0] + UNROLL - 1) // UNROLL, body, 0)


def cut_early_kernel(*refs):
    aims, blocks, (other, own, slots) = refs[:6], refs[6:8], refs[8:]
    fill_slots(EARLY, blocks, slots)
    for i, wins in enumerate((other, own)):
        wins[...] = jnp.zeros_like(wins)
        cut_windows(*aims[3 * i : 3 * i + 3], slots, wins)


def cut_other_kernel(base, lane, listed, early, *refs):
    blocks, (wins, slots) = refs[:2], refs[2:]
    fill_slots(LATE, blocks, slots)
    wins[...] = early[...]
    cut_windows(base, lane, listed, slots, wins)


def cut_own_kernel(base, lane, listed, early, slots, wins):
    wins[...] = early[...]
    cut_windows(base, lane, listed, slots, wins)


WINDOWS = jax.ShapeDtypeStruct((SAMPLES, LANES), F32)


def cut(kernel, aims, arrays, out_shape, scratch=()):
    smem = pl.BlockSpec(memory_space=pltpu.SMEM)
    vmem = pl.BlockSpec(memory_space=pltpu.VMEM)
    return pl.pallas_call(
        kernel,
        out_shape=out_shape,
        in_specs=[smem] * len(aims) + [vmem] * len(arrays),
        out_specs=[vmem] * len(out_shape),
        scratch_shapes=scratch,
        compiler_params=pltpu.CompilerParams(vmem_limit_bytes=8 << 20),
        cost_estimate=pl.CostEstimate(flops=1 << 20, bytes_accessed=6 << 20, transcendentals=0),
        name=kernel.__name__,
    )(*aims, *arrays)


def shrink_kernel(cutoff, est, here, there, table, result, out, sems):
    tables = [
        table.at[pl.ds(0, 512), :],
        table.at[pl.ds(512, 512), :],
        table.at[pl.ds(1024, 256), pl.ds(0, 256)],
        table.at[pl.ds(1024, 256), pl.ds(256, 256)],
        table.at[pl.ds(1280, 256), pl.ds(0, 384)],
        table.at[pl.ds(1536, 256), pl.ds(0, 384)],
    ]
    fwd, bwd = table.at[pl.ds(1792, 512), pl.ds(0, 256)], table.at[pl.ds(1792, 512), pl.ds(256, 256)]
    stepped = jnp.concatenate(
        [
            est[:, pl.ds(t * LANES, LANES)] - 0.5 * (here[pl.ds(t * SHOTS, SHOTS), :] + there[pl.ds(t * SHOTS, SHOTS), :])
            for t in range(TILES)
        ],
        axis=1,
    )
    front, rear = stepped[:, :512], stepped[:, 512:]
    folded = front + rear
    odd = times(front - rear, tables[0], tables[1])
    mid = times(folded[:, :256] - folded[:, 256:], tables[2], tables[3])
    even = times(folded[:, :256] + folded[:, 256:], tables[4], tables[5])
    last = even[:, 2 * PAIR :]
    stacked = jnp.concatenate(
        [
            jnp.concatenate([odd[:, :ODD], mid[:, :PAIR], even[:, :PAIR], last], axis=1),
            jnp.concatenate(
                [odd[:, ODD:], mid[:, PAIR:], even[:, PAIR : 2 * PAIR], jnp.zeros_like(last)], axis=1
            ),
        ],
        axis=0,
    )
    coeff = mix(fwd, stacked)
    real, imag = coeff[:SHOTS], coeff[SHOTS:]
    level = cutoff[0] * 128.0
    power = real * real + imag * imag
    factor = 1.0 - level * lax.rsqrt(jnp.maximum(power, level * level))
    column = lax.broadcasted_iota(jnp.int32, real.shape, 1)
    weight = jnp.where((column == ODD + PAIR) | (column >= ODD + 2 * PAIR), 1.0, 2.0)
    factor = factor * weight * (1.0 / (PATCH * SAMPLES))
    back = mix(bwd, jnp.concatenate([real * factor, imag * factor], axis=0))
    real, imag = back[:SHOTS], back[SHOTS:]
    mid = times_t(
        jnp.concatenate([real[:, ODD : ODD + PAIR], imag[:, ODD : ODD + PAIR]], axis=1),
        tables[2],
        tables[3],
    )
    even = times_t(
        jnp.concatenate(
            [
                real[:, ODD + PAIR : ODD + 2 * PAIR],
                imag[:, ODD + PAIR : ODD + 2 * PAIR],
                real[:, ODD + 2 * PAIR :],
            ],
            axis=1,
        ),
        tables[4],
        tables[5],
    )
    spectrum = split(jnp.concatenate([real[:, :ODD], imag[:, :ODD]], axis=1))
    copies = []
    for part, front in enumerate((even + mid, even - mid)):
        spots = pl.ds(part * 2 * PAIR, 2 * PAIR)
        odd = split_times_t(spectrum, tables[0].at[spots, :], tables[1].at[spots, :])
        for sign, value in enumerate((front + odd, front - odd)):
            spots = pl.ds(sign * 512 + part * 2 * PAIR, 2 * PAIR)
            out[:, spots] = value
            copies.append(
                pltpu.make_async_copy(out.at[:, spots], result.at[:, spots], sems.at[part * 2 + sign])
            )
            copies[-1].start()
    for copy in copies:
        copy.wait()


def shrink(cutoff, est, here, there):
    vmem = pl.BlockSpec(memory_space=pltpu.VMEM)
    return pl.pallas_call(
        shrink_kernel,
        out_shape=jax.ShapeDtypeStruct((SHOTS, SAMPLES), F32),
        in_specs=[pl.BlockSpec(memory_space=pltpu.SMEM)] + [vmem] * 4,
        out_specs=pl.BlockSpec(memory_space=pl.ANY),
        scratch_shapes=[pltpu.VMEM((SHOTS, SAMPLES), F32), pltpu.SemaphoreType.DMA((4,))],
        compiler_params=pltpu.CompilerParams(vmem_limit_bytes=12 << 20),
        cost_estimate=pl.CostEstimate(flops=1 << 29, bytes_accessed=8 << 20, transcendentals=0),
        name="shrink",
    )(cutoff, est, here, there, jnp.asarray(all_tables()))


def shards(record, estimate, launch_portion, launch_offset, threshold):
    index = lax.axis_index("seg")
    core, y, x = index & 1, (index >> 1) & 3, index >> 3
    first, second = jnp.where(core == 0, x, y), jnp.where(core == 0, y, x)
    record = record.reshape(SEG_ROWS, LANES)
    spot = second.reshape(1)

    other = swap_cores(estimate)
    rows, firing = fetch(estimate, launch_portion.reshape(1, SHOTS), launch_offset.reshape(1, SHOTS))
    other_firing = swap_cores(launch_portion)[:, 0] * (SEG_ROWS * LANES) + swap_cores(launch_offset)
    own_aims = aims(firing, first, second, core)
    other_aims = aims(other_firing, first, second, core)
    base, lane = [jnp.concatenate([a[:SHOTS], b]) for a, b in zip(own_aims, other_aims)]
    shots = (base, lane, spot, join(other, rows))

    (opposite,) = place(3, 1, *shots)
    opposite = swap(opposite, 2, True)
    one, three = place(1, 2, *shots)
    (column,) = place(0, 1, *shots, record, opposite)
    column = column + swap(one, 1, True) + swap(three, 3, True)
    arrived = [swap(column, k, False) for k in (2, 1, 3)]
    column = column + arrived[0] + arrived[1] + arrived[2]

    residual, *lists = side(spot, (other_aims[0], own_aims[0]), column)
    far_blocks = {k: swap(column, k, True) for k in (2, 1, 3)}

    far_blocks[0] = column

    others, owns = cut(
        cut_early_kernel,
        (*other_aims, lists[0], *own_aims, lists[2]),
        [far_blocks[k] for k in EARLY],
        [WINDOWS] * 2,
        [pltpu.VMEM(SLOTS.shape, F32)],
    )
    late = [far_blocks[k] for k in LATE]
    others, slots = cut(cut_other_kernel, (*other_aims, lists[1]), [others, *late], [WINDOWS, SLOTS])
    there = swap_cores(others)
    (here,) = cut(cut_own_kernel, (*own_aims, lists[3]), [owns, slots], [WINDOWS])
    updated = shrink(threshold, estimate, here, there)
    return (updated, residual.reshape(-1))


def solution(mesh):
    placed = (P(("node", "seg")), P(("node", "seg"), None), P("seg", None), P("seg"), P())
    return jax.shard_map(
        shards,
        mesh=mesh,
        in_specs=placed,
        out_specs=(P(("node", "seg"), None), P(("node", "seg"))),
        check_vma=False,
    )
```

```python
import math

import jax
import jax.numpy as jnp
import ml_dtypes
import numpy as np
from jax import lax
from jax.experimental import pallas as pl
from jax.experimental.pallas import tpu as pltpu
from jax.sharding import PartitionSpec as P

PATCH = 16
LANES = 128
SIDE = 4
SEGS = 32
SEG_ROWS = 256
SLOT = SEG_ROWS + 24
SPARE = SIDE * SIDE * SLOT
SHOTS = 128
BOTH = 2 * SHOTS
UNROLL = 32
ORDER = (0, 1, 3, 2)
SAMPLES = 1024
TILES = SAMPLES // LANES
ODD = 256
PAIR = 128
F32 = jnp.float32
BF16 = jnp.bfloat16


def seg_index(x, y, core):
    return (x * SIDE + y) * 2 + core


def swap_pairs(step, first):
    pairs = []
    for x in range(SIDE):
        for y in range(SIDE):
            for core in range(2):
                along_x = (core == 0) == first
                to = seg_index(x ^ step, y, core) if along_x else seg_index(x, y ^ step, core)
                pairs.append((seg_index(x, y, core), to))
    return pairs


def swap(value, step, first):
    return lax.ppermute(value, "seg", swap_pairs(step, first))


def swap_cores(value):
    return lax.ppermute(value, "seg", [(i, i ^ 1) for i in range(SEGS)])


def split(value):
    high = value.astype(BF16)
    return high, (value - high.astype(F32)).astype(BF16)


def np_split(value):
    value = value.astype(np.float32)
    high = value.astype(ml_dtypes.bfloat16)
    return high, (value - high.astype(np.float32)).astype(ml_dtypes.bfloat16)


def waves(samples, bins):
    phase = np.outer(np.arange(samples), np.asarray(bins)) % SAMPLES
    angle = phase * (2.0 * math.pi / SAMPLES)
    return [np.cos(angle), -np.sin(angle)]


def time_tables():
    odd = waves(2 * ODD, 2 * np.arange(ODD) + 1)
    mid = waves(2 * PAIR, 4 * np.arange(PAIR) + 2)
    even = waves(2 * PAIR, 4 * np.arange(PAIR))
    last = np.zeros((2 * PAIR, LANES))
    last[:, 0] = 1.0 - 2.0 * (np.arange(2 * PAIR) % 2)
    blank = np.zeros((2 * PAIR, LANES))
    return [np.concatenate(t, axis=1) for t in (odd, mid, even + [last, blank])]


def patch_table():
    phase = np.outer(np.arange(PATCH), np.arange(PATCH)) % PATCH
    angle = phase * (2.0 * math.pi / PATCH)
    blocks = np.eye(SHOTS // PATCH)
    cos, sin = np.kron(blocks, np.cos(angle)), np.kron(blocks, np.sin(angle))
    return np.block([[cos, sin], [-sin, cos]])


def all_tables():
    odd, mid, even = [np_split(table) for table in time_tables()]
    forward, backward = np_split(patch_table()), np_split(patch_table().T)
    patch = np.concatenate([np.concatenate(forward), np.concatenate(backward)], axis=1)
    return np.concatenate([*odd, np.concatenate(mid, axis=1), *even, patch])


def fetch_kernel(source, portion, offset, rows, portion_out, offset_out, sems):
    copies = [(portion, portion_out), (offset, offset_out)]
    for tile in range(TILES):
        copies.append((source.at[:, pl.ds(tile * LANES, LANES)], rows.at[pl.ds(tile * SHOTS, SHOTS)]))
    copies = [pltpu.make_async_copy(*pair, sems.at[i]) for i, pair in enumerate(copies)]
    for copy in copies:
        copy.start()
    for copy in copies:
        copy.wait()


ROWS = jax.ShapeDtypeStruct((SAMPLES, LANES), F32)


def fetch(source, portion, offset):
    inputs = [pltpu.with_memory_space_constraint(x, pltpu.HBM) for x in (source, portion, offset)]
    whens = jax.ShapeDtypeStruct((1, SHOTS), jnp.int32)
    rows, portion, offset = pl.pallas_call(
        fetch_kernel,
        out_shape=[ROWS, whens, whens],
        in_specs=[pl.BlockSpec(memory_space=pltpu.HBM)] * 3,
        out_specs=[pl.BlockSpec(memory_space=pltpu.VMEM)] * 3,
        scratch_shapes=[pltpu.SemaphoreType.DMA((TILES + 2,))],
        compiler_params=pltpu.CompilerParams(vmem_limit_bytes=4 << 20),
        cost_estimate=pl.CostEstimate(flops=1 << 10, bytes_accessed=1 << 20, transcendentals=0),
        name="fetch_shots",
    )(*inputs)
    return rows, portion[0] * (SEG_ROWS * LANES) + offset[0]


def join_kernel(other, own, rows):
    rows[pl.ds(0, SAMPLES), :] = own[...]
    for tile in range(TILES):
        rows[pl.ds(SAMPLES + tile * SHOTS, SHOTS), :] = other[:, pl.ds(tile * LANES, LANES)]


def join(other, own):
    vmem = pl.BlockSpec(memory_space=pltpu.VMEM)
    return pl.pallas_call(
        join_kernel,
        out_shape=jax.ShapeDtypeStruct((2 * SAMPLES, LANES), F32),
        in_specs=[vmem] * 2,
        out_specs=vmem,
        compiler_params=pltpu.CompilerParams(vmem_limit_bytes=4 << 20),
        cost_estimate=pl.CostEstimate(flops=1, bytes_accessed=1, transcendentals=0),
        name="join_shots",
    )(other, own)


def place_kernel(first, count, rows, base, lane, counts, spot, *refs):
    outs, (acc, listed) = refs[-2 - count : -2], refs[-2:]
    low_end, high_end = first * SIDE * SLOT, (first + count) * SIDE * SLOT
    acc[...] = jnp.zeros_like(acc)

    def note(shot, number):
        listed[number] = shot
        return number + counts[shot]

    number = lax.fori_loop(0, BOTH, note, 0, unroll=16)
    for i in range(UNROLL):
        listed[number + i] = BOTH
    lanes = lax.broadcasted_iota(jnp.int32, (8, LANES), 1)
    top = lax.broadcasted_iota(jnp.int32, (8, LANES), 0) == 0

    def body(n, carry):
        work = []
        for u in range(UNROLL):
            shot = listed[n * UNROLL + u]
            row = ((shot >> 7) & 1) * SAMPLES + (shot & (SHOTS - 1))
            turn = lane[shot]
            value = pltpu.roll(rows[pl.ds(row, TILES, stride=SHOTS), :], turn, 1)
            here = lanes >= turn
            next_row = pltpu.roll(jnp.where(here, 0.0, value), 1, 0)
            low = jnp.where(here, value, 0.0) + jnp.where(top, 0.0, next_row)
            start = jnp.where(shot == BOTH, high_end + 8, base[shot]) - low_end
            work.append((start, low, jnp.where(top, next_row, 0.0)))
        for start, low, high in work:
            acc[pl.ds(start, 8), :] += low
            acc[pl.ds(start + 8, 8), :] += high
        return carry

    lax.fori_loop(0, (number + UNROLL - 1) // UNROLL, body, 0)
    for k in range(count):
        for m in range(SIDE):
            slot, spots = pl.ds((k * SIDE + m) * SLOT + 8, SEG_ROWS), pl.ds(m * SEG_ROWS, SEG_ROWS)
            if ORDER[first] == 0:
                outs[k][spots, :] = acc[slot, :] + refs[1][spots, :]
            else:
                outs[k][spots, :] = acc[slot, :]
    if ORDER[first] == 0:
        mine = pl.ds(pl.multiple_of(spot[0] * SEG_ROWS, SEG_ROWS), SEG_ROWS)
        outs[0][mine, :] -= refs[0][...]


def place(first, count, base, lane, spot, rows, *extra):
    low_end, high_end = first * SIDE * SLOT, (first + count) * SIDE * SLOT
    counts = ((base >= low_end) & (base < high_end)).astype(jnp.int32)
    smem = pl.BlockSpec(memory_space=pltpu.SMEM)
    vmem = pl.BlockSpec(memory_space=pltpu.VMEM)

    def kernel(*refs):
        place_kernel(first, count, *refs)

    return pl.pallas_call(
        kernel,
        out_shape=[jax.ShapeDtypeStruct((SIDE * SEG_ROWS, LANES), F32)] * count,
        in_specs=[vmem] + [smem] * 4 + [vmem] * len(extra),
        out_specs=[vmem] * count,
        scratch_shapes=[
            pltpu.VMEM((count * SIDE * SLOT + 32, LANES), F32),
            pltpu.SMEM((BOTH + UNROLL,), jnp.int32),
        ],
        compiler_params=pltpu.CompilerParams(vmem_limit_bytes=8 << 20),
        cost_estimate=pl.CostEstimate(flops=1 << 20, bytes_accessed=8 << 20, transcendentals=0),
        name=f"place_shots_{first}",
    )(rows, base, lane, counts, spot, *extra)


SLOTS = jax.ShapeDtypeStruct((SPARE + 32, LANES), F32)


def aims(firing, first, second, core):
    seg, row = firing >> 15, (firing >> 7) & (SEG_ROWS - 1)
    inside = (seg & 1) == core
    kept = inside | ((row >= SEG_ROWS - 8) & (seg < SEGS - 1))
    seg = jnp.where(inside, seg, seg + 1)
    row = jnp.where(inside, row, row - SEG_ROWS)
    x, y = seg >> 3, (seg >> 1) & 3
    to_first = jnp.where(core == 0, x, y)
    to_second = jnp.where(core == 0, y, x)
    away = to_first ^ first
    slot = jnp.where(away >= 2, 5 - away, away) * SIDE + to_second
    base = jnp.where(kept, slot * SLOT + 8 + row, -1)
    base = jnp.concatenate([base, jnp.full((8,), SPARE + 8, jnp.int32)])
    return base, jnp.concatenate([firing & (LANES - 1), jnp.zeros((8,), jnp.int32)])


def times(value, high, low):
    a, b = split(value)
    both = jnp.dot(jnp.concatenate([a, b], axis=0), high[...], preferred_element_type=F32)
    return both[:SHOTS] + both[SHOTS:] + jnp.dot(a, low[...], preferred_element_type=F32)


def times_t(value, high, low):
    return split_times_t(split(value), high, low)


def split_times_t(value, high, low):
    def one(x, y):
        return lax.dot_general(x, y, (((1,), (1,)), ((), ())), preferred_element_type=F32)

    both = one(jnp.concatenate(value, axis=0), high[...])
    return both[:SHOTS] + both[SHOTS:] + one(value[0], low[...])


def mix(table, value):
    a, b = split(value)
    both = jnp.dot(table[...], a, preferred_element_type=F32)
    return both[:BOTH] + both[BOTH:] + jnp.dot(table[pl.ds(0, BOTH), :], b, preferred_element_type=F32)


EARLY, LATE = (0, 2), (1, 3)


def side_kernel(column, spot, *refs):
    count = (len(refs) - 1) // 2
    flags, residual, lists = refs[:count], refs[count], refs[count + 1 :]
    own = pl.ds(pl.multiple_of(spot[0] * SEG_ROWS, SEG_ROWS), SEG_ROWS)
    residual[...] = -column[own, :]
    for flag, listed in zip(flags, lists):

        def note(shot, count, flag=flag, listed=listed):
            listed[count] = shot
            return count + flag[shot]

        count = lax.fori_loop(0, SHOTS, note, 1, unroll=8)
        for i in range(UNROLL):
            listed[count + i] = listed[jnp.maximum(count - 1, 1)]
        listed[0] = count - 1


def side(spot, bases, column):
    smem = pl.BlockSpec(memory_space=pltpu.SMEM)
    vmem = pl.BlockSpec(memory_space=pltpu.VMEM)
    listed = jax.ShapeDtypeStruct((SHOTS + UNROLL + 8,), jnp.int32)
    flags = []
    for base in bases:
        late = (base >= SIDE * SLOT) & (base < 3 * SIDE * SLOT)
        flags += [((base >= 0) & ~late).astype(jnp.int32), late.astype(jnp.int32)]
    return pl.pallas_call(
        side_kernel,
        out_shape=[jax.ShapeDtypeStruct((SEG_ROWS, LANES), F32)] + [listed] * len(flags),
        in_specs=[vmem] + [smem] * (1 + len(flags)),
        out_specs=[vmem] + [smem] * len(flags),
        compiler_params=pltpu.CompilerParams(vmem_limit_bytes=2 << 20),
        cost_estimate=pl.CostEstimate(flops=1 << 20, bytes_accessed=8 << 20, transcendentals=0),
        name="residual_and_lists",
    )(column, spot, *flags)


def fill_slots(columns, blocks, slots):
    for k, block in zip(columns, blocks):
        for m in range(SIDE):
            start = (ORDER.index(k) * SIDE + m) * SLOT
            slots[pl.ds(start, 8), :] = jnp.zeros((8, LANES), F32)
            slots[pl.ds(start + 8, SEG_ROWS), :] = block[pl.ds(m * SEG_ROWS, SEG_ROWS), :]
            slots[pl.ds(start + 8 + SEG_ROWS, 16), :] = jnp.zeros((16, LANES), F32)


def cut_windows(base, lane, listed, slots, wins):
    lanes = lax.broadcasted_iota(jnp.int32, (8, LANES), 1)

    def body(n, carry):
        work = []
        for u in range(UNROLL):
            shot = listed[1 + n * UNROLL + u]
            start, turn = base[shot], lane[shot]
            window = jnp.where(lanes >= turn, slots[pl.ds(start, 8), :], slots[pl.ds(start + 1, 8), :])
            work.append((shot, pltpu.roll(window, (LANES - turn) & (LANES - 1), 1)))
        for shot, window in work:
            wins[pl.ds(shot, TILES, stride=SHOTS), :] = window
        return carry

    lax.fori_loop(0, (listed[0] + UNROLL - 1) // UNROLL, body, 0)


def cut_early_kernel(*refs):
    aims, blocks, (other, own, slots) = refs[:6], refs[6:8], refs[8:]
    fill_slots(EARLY, blocks, slots)
    for i, wins in enumerate((other, own)):
        wins[...] = jnp.zeros_like(wins)
        cut_windows(*aims[3 * i : 3 * i + 3], slots, wins)


def cut_other_kernel(base, lane, listed, early, *refs):
    blocks, (wins, slots) = refs[:2], refs[2:]
    fill_slots(LATE, blocks, slots)
    wins[...] = early[...]
    cut_windows(base, lane, listed, slots, wins)


def cut_own_kernel(base, lane, listed, early, slots, wins):
    wins[...] = early[...]
    cut_windows(base, lane, listed, slots, wins)


WINDOWS = jax.ShapeDtypeStruct((SAMPLES, LANES), F32)


def cut(kernel, aims, arrays, out_shape, scratch=()):
    smem = pl.BlockSpec(memory_space=pltpu.SMEM)
    vmem = pl.BlockSpec(memory_space=pltpu.VMEM)
    return pl.pallas_call(
        kernel,
        out_shape=out_shape,
        in_specs=[smem] * len(aims) + [vmem] * len(arrays),
        out_specs=[vmem] * len(out_shape),
        scratch_shapes=scratch,
        compiler_params=pltpu.CompilerParams(vmem_limit_bytes=8 << 20),
        cost_estimate=pl.CostEstimate(flops=1 << 20, bytes_accessed=6 << 20, transcendentals=0),
        name=kernel.__name__,
    )(*aims, *arrays)


def shrink_kernel(cutoff, est, here, there, table, result, out, sems):
    tables = [
        table.at[pl.ds(0, 512), :],
        table.at[pl.ds(512, 512), :],
        table.at[pl.ds(1024, 256), pl.ds(0, 256)],
        table.at[pl.ds(1024, 256), pl.ds(256, 256)],
        table.at[pl.ds(1280, 256), pl.ds(0, 384)],
        table.at[pl.ds(1536, 256), pl.ds(0, 384)],
    ]
    fwd, bwd = table.at[pl.ds(1792, 512), pl.ds(0, 256)], table.at[pl.ds(1792, 512), pl.ds(256, 256)]
    stepped = jnp.concatenate(
        [
            est[:, pl.ds(t * LANES, LANES)] - 0.5 * (here[pl.ds(t * SHOTS, SHOTS), :] + there[pl.ds(t * SHOTS, SHOTS), :])
            for t in range(TILES)
        ],
        axis=1,
    )
    front, rear = stepped[:, :512], stepped[:, 512:]
    folded = front + rear
    odd = times(front - rear, tables[0], tables[1])
    mid = times(folded[:, :256] - folded[:, 256:], tables[2], tables[3])
    even = times(folded[:, :256] + folded[:, 256:], tables[4], tables[5])
    last = even[:, 2 * PAIR :]
    stacked = jnp.concatenate(
        [
            jnp.concatenate([odd[:, :ODD], mid[:, :PAIR], even[:, :PAIR], last], axis=1),
            jnp.concatenate(
                [odd[:, ODD:], mid[:, PAIR:], even[:, PAIR : 2 * PAIR], jnp.zeros_like(last)], axis=1
            ),
        ],
        axis=0,
    )
    coeff = mix(fwd, stacked)
    real, imag = coeff[:SHOTS], coeff[SHOTS:]
    level = cutoff[0] * 128.0
    power = real * real + imag * imag
    factor = 1.0 - level * lax.rsqrt(jnp.maximum(power, level * level))
    column = lax.broadcasted_iota(jnp.int32, real.shape, 1)
    weight = jnp.where((column == ODD + PAIR) | (column >= ODD + 2 * PAIR), 1.0, 2.0)
    factor = factor * weight * (1.0 / (PATCH * SAMPLES))
    back = mix(bwd, jnp.concatenate([real * factor, imag * factor], axis=0))
    real, imag = back[:SHOTS], back[SHOTS:]
    mid = times_t(
        jnp.concatenate([real[:, ODD : ODD + PAIR], imag[:, ODD : ODD + PAIR]], axis=1),
        tables[2],
        tables[3],
    )
    even = times_t(
        jnp.concatenate(
            [
                real[:, ODD + PAIR : ODD + 2 * PAIR],
                imag[:, ODD + PAIR : ODD + 2 * PAIR],
                real[:, ODD + 2 * PAIR :],
            ],
            axis=1,
        ),
        tables[4],
        tables[5],
    )
    spectrum = split(jnp.concatenate([real[:, :ODD], imag[:, :ODD]], axis=1))
    copies = []
    for part, front in enumerate((even + mid, even - mid)):
        spots = pl.ds(part * 2 * PAIR, 2 * PAIR)
        odd = split_times_t(spectrum, tables[0].at[spots, :], tables[1].at[spots, :])
        for sign, value in enumerate((front + odd, front - odd)):
            spots = pl.ds(sign * 512 + part * 2 * PAIR, 2 * PAIR)
            out[:, spots] = value
            copies.append(
                pltpu.make_async_copy(out.at[:, spots], result.at[:, spots], sems.at[part * 2 + sign])
            )
            copies[-1].start()
    for copy in copies:
        copy.wait()


def shrink(cutoff, est, here, there):
    vmem = pl.BlockSpec(memory_space=pltpu.VMEM)
    return pl.pallas_call(
        shrink_kernel,
        out_shape=jax.ShapeDtypeStruct((SHOTS, SAMPLES), F32),
        in_specs=[pl.BlockSpec(memory_space=pltpu.SMEM)] + [vmem] * 4,
        out_specs=pl.BlockSpec(memory_space=pl.ANY),
        scratch_shapes=[pltpu.VMEM((SHOTS, SAMPLES), F32), pltpu.SemaphoreType.DMA((4,))],
        compiler_params=pltpu.CompilerParams(vmem_limit_bytes=12 << 20),
        cost_estimate=pl.CostEstimate(flops=1 << 29, bytes_accessed=8 << 20, transcendentals=0),
        name="shrink",
    )(cutoff, est, here, there, jnp.asarray(all_tables()))


def shards(record, estimate, launch_portion, launch_offset, threshold):
    index = lax.axis_index("seg")
    core, y, x = index & 1, (index >> 1) & 3, index >> 3
    first, second = jnp.where(core == 0, x, y), jnp.where(core == 0, y, x)
    record = record.reshape(SEG_ROWS, LANES)
    spot = second.reshape(1)

    other = swap_cores(estimate)
    rows, firing = fetch(estimate, launch_portion.reshape(1, SHOTS), launch_offset.reshape(1, SHOTS))
    other_firing = swap_cores(launch_portion)[:, 0] * (SEG_ROWS * LANES) + swap_cores(launch_offset)
    own_aims = aims(firing, first, second, core)
    other_aims = aims(other_firing, first, second, core)
    base, lane = [jnp.concatenate([a[:SHOTS], b]) for a, b in zip(own_aims, other_aims)]
    shots = (base, lane, spot, join(other, rows))

    (opposite,) = place(3, 1, *shots)
    opposite = swap(opposite, 2, True)
    one, three = place(1, 2, *shots)
    (column,) = place(0, 1, *shots, record, opposite)
    column = column + swap(one, 1, True) + swap(three, 3, True)
    arrived = [swap(column, k, False) for k in (2, 1, 3)]
    column = column + arrived[0] + arrived[1] + arrived[2]

    residual, *lists = side(spot, (other_aims[0], own_aims[0]), column)
    far_blocks = {k: swap(column, k, True) for k in (2, 1, 3)}

    far_blocks[0] = column

    others, owns = cut(
        cut_early_kernel,
        (*other_aims, lists[0], *own_aims, lists[2]),
        [far_blocks[k] for k in EARLY],
        [WINDOWS] * 2,
        [pltpu.VMEM(SLOTS.shape, F32)],
    )
    late = [far_blocks[k] for k in LATE]
    others, slots = cut(cut_other_kernel, (*other_aims, lists[1]), [others, *late], [WINDOWS, SLOTS])
    there = swap_cores(others)
    (here,) = cut(cut_own_kernel, (*own_aims, lists[3]), [owns, slots], [WINDOWS])
    updated = shrink(threshold, estimate, here, there)
    return (updated, residual.reshape(-1))


def solution(mesh):
    placed = (P(("node", "seg")), P(("node", "seg"), None), P("seg", None), P("seg"), P())
    return jax.shard_map(
        shards,
        mesh=mesh,
        in_specs=placed,
        out_specs=(P(("node", "seg"), None), P(("node", "seg"))),
        check_vma=False,
    )
```

```python
import math

import jax
import jax.numpy as jnp
import ml_dtypes
import numpy as np
from jax import lax
from jax.experimental import pallas as pl
from jax.experimental.pallas import tpu as pltpu
from jax.sharding import PartitionSpec as P

PATCH = 16
LANES = 128
SIDE = 4
SEGS = 32
SEG_ROWS = 256
SLOT = SEG_ROWS + 24
SPARE = SIDE * SIDE * SLOT
SHOTS = 128
BOTH = 2 * SHOTS
UNROLL = 32
ORDER = (0, 1, 3, 2)
SAMPLES = 1024
TILES = SAMPLES // LANES
ODD = 256
PAIR = 128
F32 = jnp.float32
BF16 = jnp.bfloat16


def seg_index(x, y, core):
    return (x * SIDE + y) * 2 + core


def swap_pairs(step, first):
    pairs = []
    for x in range(SIDE):
        for y in range(SIDE):
            for core in range(2):
                along_x = (core == 0) == first
                to = seg_index(x ^ step, y, core) if along_x else seg_index(x, y ^ step, core)
                pairs.append((seg_index(x, y, core), to))
    return pairs


def swap(value, step, first):
    return lax.ppermute(value, "seg", swap_pairs(step, first))


def swap_cores(value):
    return lax.ppermute(value, "seg", [(i, i ^ 1) for i in range(SEGS)])


def split(value):
    high = value.astype(BF16)
    return high, (value - high.astype(F32)).astype(BF16)


def np_split(value):
    value = value.astype(np.float32)
    high = value.astype(ml_dtypes.bfloat16)
    return high, (value - high.astype(np.float32)).astype(ml_dtypes.bfloat16)


def waves(samples, bins):
    phase = np.outer(np.arange(samples), np.asarray(bins)) % SAMPLES
    angle = phase * (2.0 * math.pi / SAMPLES)
    return [np.cos(angle), -np.sin(angle)]


def time_tables():
    odd = waves(2 * ODD, 2 * np.arange(ODD) + 1)
    mid = waves(2 * PAIR, 4 * np.arange(PAIR) + 2)
    even = waves(2 * PAIR, 4 * np.arange(PAIR))
    last = np.zeros((2 * PAIR, LANES))
    last[:, 0] = 1.0 - 2.0 * (np.arange(2 * PAIR) % 2)
    blank = np.zeros((2 * PAIR, LANES))
    return [np.concatenate(t, axis=1) for t in (odd, mid, even + [last, blank])]


def patch_table():
    phase = np.outer(np.arange(PATCH), np.arange(PATCH)) % PATCH
    angle = phase * (2.0 * math.pi / PATCH)
    blocks = np.eye(SHOTS // PATCH)
    cos, sin = np.kron(blocks, np.cos(angle)), np.kron(blocks, np.sin(angle))
    return np.block([[cos, sin], [-sin, cos]])


def all_tables():
    odd, mid, even = [np_split(table) for table in time_tables()]
    forward, backward = np_split(patch_table()), np_split(patch_table().T)
    patch = np.concatenate([np.concatenate(forward), np.concatenate(backward)], axis=1)
    return np.concatenate([*odd, np.concatenate(mid, axis=1), *even, patch])


def fetch_kernel(source, portion, offset, rows, portion_out, offset_out, sems):
    copies = [(portion, portion_out), (offset, offset_out)]
    for tile in range(TILES):
        copies.append((source.at[:, pl.ds(tile * LANES, LANES)], rows.at[pl.ds(tile * SHOTS, SHOTS)]))
    copies = [pltpu.make_async_copy(*pair, sems.at[i]) for i, pair in enumerate(copies)]
    for copy in copies:
        copy.start()
    for copy in copies:
        copy.wait()


ROWS = jax.ShapeDtypeStruct((SAMPLES, LANES), F32)


def fetch(source, portion, offset):
    inputs = [pltpu.with_memory_space_constraint(x, pltpu.HBM) for x in (source, portion, offset)]
    whens = jax.ShapeDtypeStruct((1, SHOTS), jnp.int32)
    rows, portion, offset = pl.pallas_call(
        fetch_kernel,
        out_shape=[ROWS, whens, whens],
        in_specs=[pl.BlockSpec(memory_space=pltpu.HBM)] * 3,
        out_specs=[pl.BlockSpec(memory_space=pltpu.VMEM)] * 3,
        scratch_shapes=[pltpu.SemaphoreType.DMA((TILES + 2,))],
        compiler_params=pltpu.CompilerParams(vmem_limit_bytes=4 << 20),
        cost_estimate=pl.CostEstimate(flops=1 << 10, bytes_accessed=1 << 20, transcendentals=0),
        name="fetch_shots",
    )(*inputs)
    return rows, portion[0] * (SEG_ROWS * LANES) + offset[0]


def join_kernel(other, own, rows):
    rows[pl.ds(0, SAMPLES), :] = own[...]
    for tile in range(TILES):
        rows[pl.ds(SAMPLES + tile * SHOTS, SHOTS), :] = other[:, pl.ds(tile * LANES, LANES)]


def join(other, own):
    vmem = pl.BlockSpec(memory_space=pltpu.VMEM)
    return pl.pallas_call(
        join_kernel,
        out_shape=jax.ShapeDtypeStruct((2 * SAMPLES, LANES), F32),
        in_specs=[vmem] * 2,
        out_specs=vmem,
        compiler_params=pltpu.CompilerParams(vmem_limit_bytes=4 << 20),
        cost_estimate=pl.CostEstimate(flops=1, bytes_accessed=1, transcendentals=0),
        name="join_shots",
    )(other, own)


def place_kernel(first, count, rows, base, lane, counts, spot, *refs):
    outs, (acc, listed) = refs[-2 - count : -2], refs[-2:]
    low_end, high_end = first * SIDE * SLOT, (first + count) * SIDE * SLOT
    acc[...] = jnp.zeros_like(acc)

    def note(shot, number):
        listed[number] = shot
        return number + counts[shot]

    number = lax.fori_loop(0, BOTH, note, 0, unroll=64)
    for i in range(UNROLL):
        listed[number + i] = BOTH
    lanes = lax.broadcasted_iota(jnp.int32, (8, LANES), 1)
    top = lax.broadcasted_iota(jnp.int32, (8, LANES), 0) == 0

    def body(n, carry):
        work = []
        for u in range(UNROLL):
            shot = listed[n * UNROLL + u]
            row = ((shot >> 7) & 1) * SAMPLES + (shot & (SHOTS - 1))
            turn = lane[shot]
            value = pltpu.roll(rows[pl.ds(row, TILES, stride=SHOTS), :], turn, 1)
            here = lanes >= turn
            next_row = pltpu.roll(jnp.where(here, 0.0, value), 1, 0)
            low = jnp.where(here, value, 0.0) + jnp.where(top, 0.0, next_row)
            start = jnp.where(shot == BOTH, high_end + 8, base[shot]) - low_end
            work.append((start, low, jnp.where(top, next_row, 0.0)))
        for start, low, high in work:
            acc[pl.ds(start, 8), :] += low
            acc[pl.ds(start + 8, 8), :] += high
        return carry

    lax.fori_loop(0, (number + UNROLL - 1) // UNROLL, body, 0)
    for k in range(count):
        for m in range(SIDE):
            slot, spots = pl.ds((k * SIDE + m) * SLOT + 8, SEG_ROWS), pl.ds(m * SEG_ROWS, SEG_ROWS)
            if ORDER[first] == 0:
                outs[k][spots, :] = acc[slot, :] + refs[1][spots, :]
            else:
                outs[k][spots, :] = acc[slot, :]
    if ORDER[first] == 0:
        mine = pl.ds(pl.multiple_of(spot[0] * SEG_ROWS, SEG_ROWS), SEG_ROWS)
        outs[0][mine, :] -= refs[0][...]


def place(first, count, base, lane, spot, rows, *extra):
    low_end, high_end = first * SIDE * SLOT, (first + count) * SIDE * SLOT
    counts = ((base >= low_end) & (base < high_end)).astype(jnp.int32)
    smem = pl.BlockSpec(memory_space=pltpu.SMEM)
    vmem = pl.BlockSpec(memory_space=pltpu.VMEM)

    def kernel(*refs):
        place_kernel(first, count, *refs)

    return pl.pallas_call(
        kernel,
        out_shape=[jax.ShapeDtypeStruct((SIDE * SEG_ROWS, LANES), F32)] * count,
        in_specs=[vmem] + [smem] * 4 + [vmem] * len(extra),
        out_specs=[vmem] * count,
        scratch_shapes=[
            pltpu.VMEM((count * SIDE * SLOT + 32, LANES), F32),
            pltpu.SMEM((BOTH + UNROLL,), jnp.int32),
        ],
        compiler_params=pltpu.CompilerParams(vmem_limit_bytes=8 << 20),
        cost_estimate=pl.CostEstimate(flops=1 << 20, bytes_accessed=8 << 20, transcendentals=0),
        name=f"place_shots_{first}",
    )(rows, base, lane, counts, spot, *extra)


SLOTS = jax.ShapeDtypeStruct((SPARE + 32, LANES), F32)


def aims(firing, first, second, core):
    seg, row = firing >> 15, (firing >> 7) & (SEG_ROWS - 1)
    inside = (seg & 1) == core
    kept = inside | ((row >= SEG_ROWS - 8) & (seg < SEGS - 1))
    seg = jnp.where(inside, seg, seg + 1)
    row = jnp.where(inside, row, row - SEG_ROWS)
    x, y = seg >> 3, (seg >> 1) & 3
    to_first = jnp.where(core == 0, x, y)
    to_second = jnp.where(core == 0, y, x)
    away = to_first ^ first
    slot = jnp.where(away >= 2, 5 - away, away) * SIDE + to_second
    base = jnp.where(kept, slot * SLOT + 8 + row, -1)
    base = jnp.concatenate([base, jnp.full((8,), SPARE + 8, jnp.int32)])
    return base, jnp.concatenate([firing & (LANES - 1), jnp.zeros((8,), jnp.int32)])


def times(value, high, low):
    a, b = split(value)
    both = jnp.dot(jnp.concatenate([a, b], axis=0), high[...], preferred_element_type=F32)
    return both[:SHOTS] + both[SHOTS:] + jnp.dot(a, low[...], preferred_element_type=F32)


def times_t(value, high, low):
    return split_times_t(split(value), high, low)


def split_times_t(value, high, low):
    def one(x, y):
        return lax.dot_general(x, y, (((1,), (1,)), ((), ())), preferred_element_type=F32)

    both = one(jnp.concatenate(value, axis=0), high[...])
    return both[:SHOTS] + both[SHOTS:] + one(value[0], low[...])


def mix(table, value):
    a, b = split(value)
    both = jnp.dot(table[...], a, preferred_element_type=F32)
    return both[:BOTH] + both[BOTH:] + jnp.dot(table[pl.ds(0, BOTH), :], b, preferred_element_type=F32)


EARLY, LATE = (0, 2), (1, 3)


def side_kernel(column, spot, *refs):
    count = (len(refs) - 1) // 2
    flags, residual, lists = refs[:count], refs[count], refs[count + 1 :]
    own = pl.ds(pl.multiple_of(spot[0] * SEG_ROWS, SEG_ROWS), SEG_ROWS)
    residual[...] = -column[own, :]
    for flag, listed in zip(flags, lists):

        def note(shot, count, flag=flag, listed=listed):
            listed[count] = shot
            return count + flag[shot]

        count = lax.fori_loop(0, SHOTS, note, 1, unroll=8)
        for i in range(UNROLL):
            listed[count + i] = listed[jnp.maximum(count - 1, 1)]
        listed[0] = count - 1


def side(spot, bases, column):
    smem = pl.BlockSpec(memory_space=pltpu.SMEM)
    vmem = pl.BlockSpec(memory_space=pltpu.VMEM)
    listed = jax.ShapeDtypeStruct((SHOTS + UNROLL + 8,), jnp.int32)
    flags = []
    for base in bases:
        late = (base >= SIDE * SLOT) & (base < 3 * SIDE * SLOT)
        flags += [((base >= 0) & ~late).astype(jnp.int32), late.astype(jnp.int32)]
    return pl.pallas_call(
        side_kernel,
        out_shape=[jax.ShapeDtypeStruct((SEG_ROWS, LANES), F32)] + [listed] * len(flags),
        in_specs=[vmem] + [smem] * (1 + len(flags)),
        out_specs=[vmem] + [smem] * len(flags),
        compiler_params=pltpu.CompilerParams(vmem_limit_bytes=2 << 20),
        cost_estimate=pl.CostEstimate(flops=1 << 20, bytes_accessed=8 << 20, transcendentals=0),
        name="residual_and_lists",
    )(column, spot, *flags)


def fill_slots(columns, blocks, slots):
    for k, block in zip(columns, blocks):
        for m in range(SIDE):
            start = (ORDER.index(k) * SIDE + m) * SLOT
            slots[pl.ds(start, 8), :] = jnp.zeros((8, LANES), F32)
            slots[pl.ds(start + 8, SEG_ROWS), :] = block[pl.ds(m * SEG_ROWS, SEG_ROWS), :]
            slots[pl.ds(start + 8 + SEG_ROWS, 16), :] = jnp.zeros((16, LANES), F32)


def cut_windows(base, lane, listed, slots, wins):
    lanes = lax.broadcasted_iota(jnp.int32, (8, LANES), 1)

    def body(n, carry):
        work = []
        for u in range(UNROLL):
            shot = listed[1 + n * UNROLL + u]
            start, turn = base[shot], lane[shot]
            window = jnp.where(lanes >= turn, slots[pl.ds(start, 8), :], slots[pl.ds(start + 1, 8), :])
            work.append((shot, pltpu.roll(window, (LANES - turn) & (LANES - 1), 1)))
        for shot, window in work:
            wins[pl.ds(shot, TILES, stride=SHOTS), :] = window
        return carry

    lax.fori_loop(0, (listed[0] + UNROLL - 1) // UNROLL, body, 0)


def cut_early_kernel(*refs):
    aims, blocks, (other, own, slots) = refs[:6], refs[6:8], refs[8:]
    fill_slots(EARLY, blocks, slots)
    for i, wins in enumerate((other, own)):
        wins[...] = jnp.zeros_like(wins)
        cut_windows(*aims[3 * i : 3 * i + 3], slots, wins)


def cut_other_kernel(base, lane, listed, early, *refs):
    blocks, (wins, slots) = refs[:2], refs[2:]
    fill_slots(LATE, blocks, slots)
    wins[...] = early[...]
    cut_windows(base, lane, listed, slots, wins)


def cut_own_kernel(base, lane, listed, early, slots, wins):
    wins[...] = early[...]
    cut_windows(base, lane, listed, slots, wins)


WINDOWS = jax.ShapeDtypeStruct((SAMPLES, LANES), F32)


def cut(kernel, aims, arrays, out_shape, scratch=()):
    smem = pl.BlockSpec(memory_space=pltpu.SMEM)
    vmem = pl.BlockSpec(memory_space=pltpu.VMEM)
    return pl.pallas_call(
        kernel,
        out_shape=out_shape,
        in_specs=[smem] * len(aims) + [vmem] * len(arrays),
        out_specs=[vmem] * len(out_shape),
        scratch_shapes=scratch,
        compiler_params=pltpu.CompilerParams(vmem_limit_bytes=8 << 20),
        cost_estimate=pl.CostEstimate(flops=1 << 20, bytes_accessed=6 << 20, transcendentals=0),
        name=kernel.__name__,
    )(*aims, *arrays)


def shrink_kernel(cutoff, est, here, there, table, result, out, sems):
    tables = [
        table.at[pl.ds(0, 512), :],
        table.at[pl.ds(512, 512), :],
        table.at[pl.ds(1024, 256), pl.ds(0, 256)],
        table.at[pl.ds(1024, 256), pl.ds(256, 256)],
        table.at[pl.ds(1280, 256), pl.ds(0, 384)],
        table.at[pl.ds(1536, 256), pl.ds(0, 384)],
    ]
    fwd, bwd = table.at[pl.ds(1792, 512), pl.ds(0, 256)], table.at[pl.ds(1792, 512), pl.ds(256, 256)]
    stepped = jnp.concatenate(
        [
            est[:, pl.ds(t * LANES, LANES)] - 0.5 * (here[pl.ds(t * SHOTS, SHOTS), :] + there[pl.ds(t * SHOTS, SHOTS), :])
            for t in range(TILES)
        ],
        axis=1,
    )
    front, rear = stepped[:, :512], stepped[:, 512:]
    folded = front + rear
    odd = times(front - rear, tables[0], tables[1])
    mid = times(folded[:, :256] - folded[:, 256:], tables[2], tables[3])
    even = times(folded[:, :256] + folded[:, 256:], tables[4], tables[5])
    last = even[:, 2 * PAIR :]
    stacked = jnp.concatenate(
        [
            jnp.concatenate([odd[:, :ODD], mid[:, :PAIR], even[:, :PAIR], last], axis=1),
            jnp.concatenate(
                [odd[:, ODD:], mid[:, PAIR:], even[:, PAIR : 2 * PAIR], jnp.zeros_like(last)], axis=1
            ),
        ],
        axis=0,
    )
    coeff = mix(fwd, stacked)
    real, imag = coeff[:SHOTS], coeff[SHOTS:]
    level = cutoff[0] * 128.0
    power = real * real + imag * imag
    factor = 1.0 - level * lax.rsqrt(jnp.maximum(power, level * level))
    column = lax.broadcasted_iota(jnp.int32, real.shape, 1)
    weight = jnp.where((column == ODD + PAIR) | (column >= ODD + 2 * PAIR), 1.0, 2.0)
    factor = factor * weight * (1.0 / (PATCH * SAMPLES))
    back = mix(bwd, jnp.concatenate([real * factor, imag * factor], axis=0))
    real, imag = back[:SHOTS], back[SHOTS:]
    mid = times_t(
        jnp.concatenate([real[:, ODD : ODD + PAIR], imag[:, ODD : ODD + PAIR]], axis=1),
        tables[2],
        tables[3],
    )
    even = times_t(
        jnp.concatenate(
            [
                real[:, ODD + PAIR : ODD + 2 * PAIR],
                imag[:, ODD + PAIR : ODD + 2 * PAIR],
                real[:, ODD + 2 * PAIR :],
            ],
            axis=1,
        ),
        tables[4],
        tables[5],
    )
    spectrum = split(jnp.concatenate([real[:, :ODD], imag[:, :ODD]], axis=1))
    copies = []
    for part, front in enumerate((even + mid, even - mid)):
        spots = pl.ds(part * 2 * PAIR, 2 * PAIR)
        odd = split_times_t(spectrum, tables[0].at[spots, :], tables[1].at[spots, :])
        for sign, value in enumerate((front + odd, front - odd)):
            spots = pl.ds(sign * 512 + part * 2 * PAIR, 2 * PAIR)
            out[:, spots] = value
            copies.append(
                pltpu.make_async_copy(out.at[:, spots], result.at[:, spots], sems.at[part * 2 + sign])
            )
            copies[-1].start()
    for copy in copies:
        copy.wait()


def shrink(cutoff, est, here, there):
    vmem = pl.BlockSpec(memory_space=pltpu.VMEM)
    return pl.pallas_call(
        shrink_kernel,
        out_shape=jax.ShapeDtypeStruct((SHOTS, SAMPLES), F32),
        in_specs=[pl.BlockSpec(memory_space=pltpu.SMEM)] + [vmem] * 4,
        out_specs=pl.BlockSpec(memory_space=pl.ANY),
        scratch_shapes=[pltpu.VMEM((SHOTS, SAMPLES), F32), pltpu.SemaphoreType.DMA((4,))],
        compiler_params=pltpu.CompilerParams(vmem_limit_bytes=12 << 20),
        cost_estimate=pl.CostEstimate(flops=1 << 29, bytes_accessed=8 << 20, transcendentals=0),
        name="shrink",
    )(cutoff, est, here, there, jnp.asarray(all_tables()))


def shards(record, estimate, launch_portion, launch_offset, threshold):
    index = lax.axis_index("seg")
    core, y, x = index & 1, (index >> 1) & 3, index >> 3
    first, second = jnp.where(core == 0, x, y), jnp.where(core == 0, y, x)
    record = record.reshape(SEG_ROWS, LANES)
    spot = second.reshape(1)

    other = swap_cores(estimate)
    rows, firing = fetch(estimate, launch_portion.reshape(1, SHOTS), launch_offset.reshape(1, SHOTS))
    other_firing = swap_cores(launch_portion)[:, 0] * (SEG_ROWS * LANES) + swap_cores(launch_offset)
    own_aims = aims(firing, first, second, core)
    other_aims = aims(other_firing, first, second, core)
    base, lane = [jnp.concatenate([a[:SHOTS], b]) for a, b in zip(own_aims, other_aims)]
    shots = (base, lane, spot, join(other, rows))

    (opposite,) = place(3, 1, *shots)
    opposite = swap(opposite, 2, True)
    one, three = place(1, 2, *shots)
    (column,) = place(0, 1, *shots, record, opposite)
    column = column + swap(one, 1, True) + swap(three, 3, True)
    arrived = [swap(column, k, False) for k in (2, 1, 3)]
    column = column + arrived[0] + arrived[1] + arrived[2]

    residual, *lists = side(spot, (other_aims[0], own_aims[0]), column)
    far_blocks = {k: swap(column, k, True) for k in (2, 1, 3)}

    far_blocks[0] = column

    others, owns = cut(
        cut_early_kernel,
        (*other_aims, lists[0], *own_aims, lists[2]),
        [far_blocks[k] for k in EARLY],
        [WINDOWS] * 2,
        [pltpu.VMEM(SLOTS.shape, F32)],
    )
    late = [far_blocks[k] for k in LATE]
    others, slots = cut(cut_other_kernel, (*other_aims, lists[1]), [others, *late], [WINDOWS, SLOTS])
    there = swap_cores(others)
    (here,) = cut(cut_own_kernel, (*own_aims, lists[3]), [owns, slots], [WINDOWS])
    updated = shrink(threshold, estimate, here, there)
    return (updated, residual.reshape(-1))


def solution(mesh):
    placed = (P(("node", "seg")), P(("node", "seg"), None), P("seg", None), P("seg"), P())
    return jax.shard_map(
        shards,
        mesh=mesh,
        in_specs=placed,
        out_specs=(P(("node", "seg"), None), P(("node", "seg"))),
        check_vma=False,
    )
```
